32 devices in a mesh: wide: 8 (over z, x), narrow: 4 (over y, core).
Axes of the slice: x: 2, y: 2, z: 4, core: 2. Of those that a mesh axis runs over, the one named last changes fastest.
Arguments:
- snapshot: float32 [512, 16, 64, 128], P('wide', 'narrow'), may hold values from -81 to 81
Outputs:
- core: float32 [256, 16, 64, 128], P(None, 'narrow', 'wide')
- factor: float32 [512, 256], replicated
The draws below stay inside these ranges and needn't reach their ends.
All inputs are finite; a program needn't handle non-finite values.
Results may differ from the reference program's by a relative error of at most 0.000071.
Values sent between devices are 32-bit elements; how exact they have to be, the bound alone decides.
No kernel may reach another device: no remote copies, remote signals or barrier semaphores. Data moves between devices by JAX's collectives and lax.ppermute only.
A program may use at most 320 MiB of HBM per device.

```python
import math
import jax
import jax.numpy as jnp
from jax import lax

NX = 512
RANK = 256
FIELDS = 128
NY = 16
NZ = 64


def draw_snapshot(key, part):
    keys = jax.random.split(jax.random.fold_in(key, 11), 4)
    noise = jnp.clip(jax.random.normal(keys[0], (NX, NY, NZ, FIELDS), jnp.float32), -6.0, 6.0)
    shared = jnp.clip(jax.random.normal(keys[3], (1, NY, NZ, FIELDS), jnp.float32), -6.0, 6.0)
    row_scale = 0.3 * jnp.exp(jax.random.uniform(keys[1], (NX, 1, 1, 1), jnp.float32, 0.0, math.log(10.0)))
    mixing = jnp.clip(0.1 * jax.random.normal(keys[2], (NX, 1, 1, 1), jnp.float32), -0.5, 0.5)
    depth = jnp.arange(NZ, dtype=jnp.float32).reshape(1, 1, NZ, 1)
    z_scale = 1.0 + 2.0 * depth / max(NZ - 1, 1)
    return row_scale * z_scale * (noise + mixing * shared)


def setup_inputs(seed: int = 0) -> dict:
    arg_keys = jax.random.split(jax.random.key(seed), 2)
    snapshot = draw_snapshot(jax.random.fold_in(arg_keys[1], 71), 0)
    return {"snapshot": snapshot}


def reference(snapshot):
    unfold = snapshot.reshape(NX, -1)
    gram = jnp.dot(unfold.astype(jnp.float32), unfold.T.astype(jnp.float32), precision=lax.Precision.HIGHEST, preferred_element_type=jnp.float32)
    upper = jnp.linalg.cholesky(gram).T
    rows_kept = upper[:RANK, :]
    lengths = jnp.sqrt(lax.optimization_barrier(jnp.sum(rows_kept * rows_kept, axis=1)))
    factor = (rows_kept / lengths[:, None]).T
    core = jnp.dot(factor.T.astype(jnp.float32), unfold.astype(jnp.float32), precision=lax.Precision.HIGHEST, preferred_element_type=jnp.float32)
    return (core.reshape(RANK, NY, NZ, FIELDS), factor)
```

```python
import functools

import jax
import jax.numpy as jnp
from jax import lax
from jax.experimental import pallas as pl
from jax.experimental.pallas import tpu as pltpu
from jax.sharding import PartitionSpec as P

RANK = 256
LANES = 128
FAST_WIDE = 8
HIGHEST = lax.Precision.HIGHEST
VMEM_LIMIT = 48 * 1024 * 1024


def swapped(flag, blocks, distance):
    return [jnp.where(flag, blocks[i ^ distance], blocks[i]) for i in range(len(blocks))]


def in_row_order(place, blocks):
    distance = 1
    while distance < len(blocks):
        blocks = swapped((place & distance) != 0, blocks, distance)
        distance *= 2
    return blocks


def two_slabs(place, refs, s):
    sides = []
    for t in (s, s + 1):
        blocks = in_row_order(place, [r[t] for r in refs])
        sides.append(jnp.concatenate(blocks, axis=0))
    return jnp.concatenate(sides, axis=1)


def rows_dot(a, b):
    return lax.dot_general(
        a, b, (((1,), (1,)), ((), ())), precision=HIGHEST, preferred_element_type=jnp.float32
    )


def own_gram_kernel(place_ref, *refs):
    blocks, out_ref = refs[:-1], refs[-1]

    @pl.when(pl.program_id(0) == 0)
    def _():
        out_ref[...] = jnp.zeros_like(out_ref)

    total = out_ref[...]
    for s in range(0, blocks[0].shape[0], 2):
        own = two_slabs(place_ref[0], blocks, s)
        total += rows_dot(own, own)
    out_ref[...] = total


def gram_kernel(place_ref, own_gram_ref, *refs):
    half = (len(refs) - 2) // 2
    own_refs, other_refs, out_ref, cross_ref = refs[:half], refs[half:-2], refs[-2], refs[-1]
    place = place_ref[0]
    first = pl.program_id(0) == 0

    @pl.when(first)
    def _():
        out_ref[...] = jnp.zeros_like(out_ref)
        cross_ref[...] = jnp.zeros_like(cross_ref)

    cross = cross_ref[...]
    total = out_ref[:RANK, :]
    for s in range(0, own_refs[0].shape[0], 2):
        own = two_slabs(place, own_refs, s)
        other = two_slabs(place, other_refs, s)
        cross += rows_dot(other, own)
        total += rows_dot(other, other)
    cross_ref[...] = cross
    out_ref[:RANK, :] = total

    @pl.when(pl.program_id(0) == pl.num_programs(0) - 1)
    def _():
        low = place < half
        out_ref[:RANK, :] = jnp.where(low, own_gram_ref[...], total)
        out_ref[RANK:, :] = jnp.where(low, cross, cross.T)


def whole(shape):
    return pl.BlockSpec(shape, lambda i: (0,) * len(shape))


def own_gram(place, blocks, steps):
    cells, rows, fields = blocks[0].shape
    part = pl.BlockSpec((cells // steps, rows, fields), lambda i: (i, 0, 0))
    size = rows * len(blocks)
    return pl.pallas_call(
        own_gram_kernel,
        grid=(steps,),
        in_specs=[pl.BlockSpec(memory_space=pltpu.SMEM)] + [part] * len(blocks),
        out_specs=whole((size, size)),
        out_shape=jax.ShapeDtypeStruct((size, size), jnp.float32),
        compiler_params=pltpu.CompilerParams(vmem_limit_bytes=VMEM_LIMIT),
        cost_estimate=pl.CostEstimate(
            flops=12 * size * size * cells * fields, bytes_accessed=4 * size * cells * fields, transcendentals=0
        ),
        name="own_gram",
    )(place, *blocks)


def full_gram(place, own, blocks, steps):
    cells, rows, fields = blocks[0].shape
    part = pl.BlockSpec((cells // steps, rows, fields), lambda i: (i, 0, 0))
    size = rows * len(blocks)
    return pl.pallas_call(
        gram_kernel,
        grid=(steps,),
        in_specs=[pl.BlockSpec(memory_space=pltpu.SMEM), whole(own.shape)] + [part] * len(blocks),
        out_specs=whole((size, RANK)),
        out_shape=jax.ShapeDtypeStruct((size, RANK), jnp.float32),
        scratch_shapes=[pltpu.VMEM((RANK, RANK), jnp.float32)],
        compiler_params=pltpu.CompilerParams(vmem_limit_bytes=VMEM_LIMIT),
        cost_estimate=pl.CostEstimate(
            flops=12 * size * RANK * cells * fields, bytes_accessed=4 * size * cells * fields, transcendentals=0
        ),
        name="full_gram",
    )(place, own, *blocks)


def over(axis, n, distance):
    return functools.partial(lax.ppermute, axis_name=axis, perm=[(i, i ^ distance) for i in range(n)])


def sum_over_all(x, wide, narrow):
    place = lax.axis_index("narrow")
    distances = [1 << b for b in range(narrow.bit_length() - 1)]
    for d in distances:
        side = (place & d) != 0
        n = x.shape[0] // 2
        keep = jnp.where(side, x[n:], x[:n])
        send = jnp.where(side, x[:n], x[n:])
        x = keep + over("narrow", narrow, d)(send)
    for b in range(wide.bit_length() - 1):
        x = x + over("wide", wide, 1 << b)(x)
    for d in reversed(distances):
        side = (place & d) != 0
        got = over("narrow", narrow, d)(x)
        x = jnp.where(side, jnp.concatenate([got, x]), jnp.concatenate([x, got]))
    return x


PANEL = 64
SUB = 8


def refine_reciprocal(d):
    r = pl.reciprocal(d, approx=True)
    r = r * (2.0 - d * r)
    return r * (2.0 - d * r)


def refine_rsqrt(d):
    r = lax.rsqrt(d)
    return r * (1.5 - 0.5 * d * r * r)


def cholesky_kernel(gram_ref, upper_ref, inverse_ref, work):
    n = gram_ref.shape[0]
    tiles = n // LANES
    sub = lax.broadcasted_iota(jnp.int32, (SUB, LANES), 0)
    lane = lax.broadcasted_iota(jnp.int32, (SUB, LANES), 1)
    row_id = lax.broadcasted_iota(jnp.int32, (n, n), 0)
    col_id = lax.broadcasted_iota(jnp.int32, (n, n), 1)
    work[:, :n] = gram_ref[...]
    work[:, n:] = jnp.where(row_id == col_id, 1.0, 0.0)
    for p in range(n // PANEL):
        top = p * PANEL
        t0 = top // LANES
        cols = [t for t in range(t0, tiles)] + [tiles + t for t in range(0, t0 + 1)]
        groups = PANEL // SUB
        grp = [
            [work[top + SUB * g : top + SUB * (g + 1), LANES * t : LANES * (t + 1)] for t in cols]
            for g in range(groups)
        ]
        pivots = [jnp.ones((SUB, LANES), jnp.float32) for _ in range(groups)]
        for i in range(PANEL):
            g0, s = divmod(i, SUB)
            c = (top + i) % LANES
            row = [jnp.broadcast_to(v[s : s + 1, :], (SUB, LANES)) for v in grp[g0]]
            d = jnp.broadcast_to(row[0][:, c : c + 1], (SUB, LANES))
            pivots[g0] = jnp.where(sub == s, d, pivots[g0])
            inv = refine_reciprocal(d)
            row = [v * inv for v in row]
            for g in range(g0, groups):
                m = jnp.broadcast_to(grp[g][0][:, c : c + 1], (SUB, LANES))
                if g == g0:
                    m = jnp.where(sub > s, m, 0.0)
                grp[g] = [v - m * r for v, r in zip(grp[g], row)]
        left = len(cols) - (t0 + 1)
        for g in range(groups):
            rs = refine_rsqrt(pivots[g])
            rows = slice(top + SUB * g, top + SUB * (g + 1))
            for v, t in zip(grp[g], cols):
                v = v * rs
                if t < tiles:
                    v = jnp.where(lane + LANES * t >= sub + (top + SUB * g), v, 0.0)
                work[rows, LANES * t : LANES * (t + 1)] = v
        for t in range(t0):
            work[top : top + PANEL, LANES * t : LANES * (t + 1)] = jnp.zeros((PANEL, LANES), jnp.float32)
        below = top + PANEL
        if below < n:
            lo, hi = LANES * t0, n + LANES * (t0 + 1)
            update = lax.dot_general(
                work[top:below, :n],
                work[top:below, lo:hi],
                (((0,), (0,)), ((), ())),
                precision=HIGHEST,
                preferred_element_type=jnp.float32,
            )
            work[below:, lo:hi] = work[below:, lo:hi] - update[below:, :]
    upper_ref[...] = work[:, :n]
    inverse_ref[...] = work[:, n:]


def cholesky(gram):
    n = gram.shape[0]
    return pl.pallas_call(
        cholesky_kernel,
        out_shape=[jax.ShapeDtypeStruct((n, n), jnp.float32)] * 2,
        scratch_shapes=[pltpu.VMEM((n, 2 * n), jnp.float32)],
        compiler_params=pltpu.CompilerParams(vmem_limit_bytes=VMEM_LIMIT),
        cost_estimate=pl.CostEstimate(flops=2 * n * n * n, bytes_accessed=12 * n * n, transcendentals=n),
        name="cholesky256",
    )(gram)


def split(x):
    high = x.astype(jnp.bfloat16)
    return high, (x - high.astype(jnp.float32)).astype(jnp.bfloat16)


def bf16_dot(a, b):
    return jnp.dot(a, b, preferred_element_type=jnp.float32)


def core_kernel(place_ref, gram_ref, upper_ref, inverse_ref, *refs):
    blocks, (out_ref, factor_ref, high, low) = refs[:-4], refs[-4:]
    place = place_ref[0]

    @pl.when(pl.program_id(0) == 0)
    def _():
        left = upper_ref[...]
        right = rows_dot(inverse_ref[...], gram_ref[...])
        squares = jnp.sum(left * left, axis=1, keepdims=True) + jnp.sum(right * right, axis=1, keepdims=True)
        length = jnp.sqrt(squares)
        rows = jnp.concatenate([left / length, right / length], axis=1)
        factor_ref[...] = rows.T
        high[...], low[...] = split(rows)

    fh, fl = high[...], low[...]
    for s in range(0, blocks[0].shape[0], 2):
        uh, ul = split(two_slabs(place, blocks, s))
        both = bf16_dot(fh, uh) + (bf16_dot(fl, uh) + bf16_dot(fh, ul))
        out_ref[:, 0, s, :] = both[:, :LANES]
        out_ref[:, 0, s + 1, :] = both[:, LANES:]


def core_and_factor(place, gram21, upper, inverse, blocks, ny, nz):
    cells, rows, fields = blocks[0].shape
    size = rows * len(blocks)
    part = pl.BlockSpec((nz, rows, fields), lambda i: (i, 0, 0))
    return pl.pallas_call(
        core_kernel,
        grid=(ny,),
        in_specs=[pl.BlockSpec(memory_space=pltpu.SMEM)]
        + [whole((RANK, RANK))] * 3
        + [part] * len(blocks),
        out_specs=[
            pl.BlockSpec((RANK, 1, nz, fields), lambda i: (0, i, 0, 0)),
            whole((size, RANK)),
        ],
        out_shape=[
            jax.ShapeDtypeStruct((RANK, ny, nz, fields), jnp.float32),
            jax.ShapeDtypeStruct((size, RANK), jnp.float32),
        ],
        scratch_shapes=[pltpu.VMEM((RANK, size), jnp.bfloat16)] * 2,
        compiler_params=pltpu.CompilerParams(vmem_limit_bytes=VMEM_LIMIT),
        cost_estimate=pl.CostEstimate(
            flops=6 * size * RANK * cells * fields,
            bytes_accessed=4 * (size + RANK) * cells * fields,
            transcendentals=0,
        ),
        name="core",
    )(place, gram21, upper, inverse, *blocks)


def tie(x, *deps):
    return lax.optimization_barrier((x,) + deps)[0]


def block_for(snapshot, device, nz):
    rows, ny, _, fields = snapshot.shape
    cut = lax.dynamic_slice_in_dim(snapshot, device * nz, nz, axis=2)
    return cut.transpose(1, 2, 0, 3).reshape(ny * nz, rows, fields)


def on_device_blocks(snapshot, wide, narrow):
    ny, nz = snapshot.shape[1], snapshot.shape[2] // wide
    here = lax.axis_index("wide")
    place = here.astype(jnp.int32).reshape(1)
    half = wide // 2
    got = {}
    send = lambda k, *deps: over("wide", wide, k)(tie(block_for(snapshot, here ^ k, nz), *deps))
    for k in (6, 4, 7, 5):
        got[k] = send(k)
    got[2] = send(2)
    got[3] = send(3, got[2])
    got[1] = send(1, got[3])
    got[0] = block_for(snapshot, here, nz)
    blocks = [got[k] for k in range(wide)]
    own = own_gram(place, blocks[:half], ny)
    gram = full_gram(place, own, blocks, ny)
    gram = sum_over_all(gram, wide, narrow)
    upper, inverse = cholesky(gram[:RANK])
    return core_and_factor(place, gram[RANK:], upper, inverse, blocks, ny, nz)


def on_device_any(snapshot):
    regrouped = lax.all_to_all(snapshot, "wide", split_axis=2, concat_axis=0, tiled=True)
    rows_all = regrouped.shape[0]
    unfold = regrouped.reshape(rows_all, -1)
    gram = lax.dot_general(
        unfold, unfold[:RANK], (((1,), (1,)), ((), ())), precision=HIGHEST, preferred_element_type=jnp.float32
    )
    gram = lax.psum(lax.psum(gram, "narrow"), "wide")
    lower = jnp.linalg.cholesky(gram[:RANK])
    upper = jnp.concatenate(
        [lower.T, lax.linalg.triangular_solve(lower, gram[RANK:].T, left_side=True, lower=True)], axis=1
    )
    lengths = jnp.sqrt(jnp.sum(upper * upper, axis=1))
    factor = (upper / lengths[:, None]).T
    core = jnp.dot(factor.T, unfold, precision=HIGHEST, preferred_element_type=jnp.float32)
    return core.reshape((RANK,) + regrouped.shape[1:]), factor


def solution(mesh):
    wide, narrow = mesh.shape["wide"], mesh.shape["narrow"]
    if wide == FAST_WIDE:
        on_device = functools.partial(on_device_blocks, wide=wide, narrow=narrow)
    else:
        on_device = on_device_any
    return jax.shard_map(
        on_device,
        mesh=mesh,
        in_specs=(P("wide", "narrow", None, None),),
        out_specs=(P(None, "narrow", "wide", None), P()),
        check_vma=False,
    )
```

```python
import functools

import jax
import jax.numpy as jnp
from jax import lax
from jax.experimental import pallas as pl
from jax.experimental.pallas import tpu as pltpu
from jax.sharding import PartitionSpec as P

RANK = 256
LANES = 128
FAST_WIDE = 8
HIGHEST = lax.Precision.HIGHEST
VMEM_LIMIT = 48 * 1024 * 1024


def swapped(flag, blocks, distance):
    return [jnp.where(flag, blocks[i ^ distance], blocks[i]) for i in range(len(blocks))]


def in_row_order(place, blocks):
    distance = 1
    while distance < len(blocks):
        blocks = swapped((place & distance) != 0, blocks, distance)
        distance *= 2
    return blocks


def two_slabs(place, refs, s):
    sides = []
    for t in (s, s + 1):
        blocks = in_row_order(place, [r[t] for r in refs])
        sides.append(jnp.concatenate(blocks, axis=0))
    return jnp.concatenate(sides, axis=1)


def rows_dot(a, b):
    return lax.dot_general(
        a, b, (((1,), (1,)), ((), ())), precision=HIGHEST, preferred_element_type=jnp.float32
    )


def own_gram_kernel(place_ref, *refs):
    blocks, out_ref = refs[:-1], refs[-1]

    @pl.when(pl.program_id(0) == 0)
    def _():
        out_ref[...] = jnp.zeros_like(out_ref)

    total = out_ref[...]
    for s in range(0, blocks[0].shape[0], 2):
        own = two_slabs(place_ref[0], blocks, s)
        total += rows_dot(own, own)
    out_ref[...] = total


def gram_kernel(place_ref, own_gram_ref, *refs):
    half = (len(refs) - 2) // 2
    own_refs, other_refs, out_ref, cross_ref = refs[:half], refs[half:-2], refs[-2], refs[-1]
    place = place_ref[0]
    first = pl.program_id(0) == 0

    @pl.when(first)
    def _():
        out_ref[...] = jnp.zeros_like(out_ref)
        cross_ref[...] = jnp.zeros_like(cross_ref)

    cross = cross_ref[...]
    total = out_ref[:RANK, :]
    for s in range(0, own_refs[0].shape[0], 2):
        own = two_slabs(place, own_refs, s)
        other = two_slabs(place, other_refs, s)
        cross += rows_dot(other, own)
        total += rows_dot(other, other)
    cross_ref[...] = cross
    out_ref[:RANK, :] = total

    @pl.when(pl.program_id(0) == pl.num_programs(0) - 1)
    def _():
        low = place < half
        out_ref[:RANK, :] = jnp.where(low, own_gram_ref[...], total)
        out_ref[RANK:, :] = jnp.where(low, cross, cross.T)


def whole(shape):
    return pl.BlockSpec(shape, lambda i: (0,) * len(shape))


def own_gram(place, blocks, steps):
    cells, rows, fields = blocks[0].shape
    part = pl.BlockSpec((cells // steps, rows, fields), lambda i: (i, 0, 0))
    size = rows * len(blocks)
    return pl.pallas_call(
        own_gram_kernel,
        grid=(steps,),
        in_specs=[pl.BlockSpec(memory_space=pltpu.SMEM)] + [part] * len(blocks),
        out_specs=whole((size, size)),
        out_shape=jax.ShapeDtypeStruct((size, size), jnp.float32),
        compiler_params=pltpu.CompilerParams(vmem_limit_bytes=VMEM_LIMIT),
        cost_estimate=pl.CostEstimate(
            flops=12 * size * size * cells * fields, bytes_accessed=4 * size * cells * fields, transcendentals=0
        ),
        name="own_gram",
    )(place, *blocks)


def full_gram(place, own, blocks, steps):
    cells, rows, fields = blocks[0].shape
    part = pl.BlockSpec((cells // steps, rows, fields), lambda i: (i, 0, 0))
    size = rows * len(blocks)
    return pl.pallas_call(
        gram_kernel,
        grid=(steps,),
        in_specs=[pl.BlockSpec(memory_space=pltpu.SMEM), whole(own.shape)] + [part] * len(blocks),
        out_specs=whole((size, RANK)),
        out_shape=jax.ShapeDtypeStruct((size, RANK), jnp.float32),
        scratch_shapes=[pltpu.VMEM((RANK, RANK), jnp.float32)],
        compiler_params=pltpu.CompilerParams(vmem_limit_bytes=VMEM_LIMIT),
        cost_estimate=pl.CostEstimate(
            flops=12 * size * RANK * cells * fields, bytes_accessed=4 * size * cells * fields, transcendentals=0
        ),
        name="full_gram",
    )(place, own, *blocks)


def over(axis, n, distance):
    return functools.partial(lax.ppermute, axis_name=axis, perm=[(i, i ^ distance) for i in range(n)])


def sum_over_all(x, wide, narrow):
    place = lax.axis_index("narrow")
    distances = [1 << b for b in range(narrow.bit_length() - 1)]
    for d in distances:
        side = (place & d) != 0
        n = x.shape[0] // 2
        keep = jnp.where(side, x[n:], x[:n])
        send = jnp.where(side, x[:n], x[n:])
        x = keep + over("narrow", narrow, d)(send)
    for b in range(wide.bit_length() - 1):
        x = x + over("wide", wide, 1 << b)(x)
    for d in reversed(distances):
        side = (place & d) != 0
        got = over("narrow", narrow, d)(x)
        x = jnp.where(side, jnp.concatenate([got, x]), jnp.concatenate([x, got]))
    return x


PANEL = 64
SUB = 8


def refine_rsqrt(d):
    r = lax.rsqrt(d)
    return r * (1.5 - 0.5 * d * r * r)


def from_row(v, i):
    return jnp.broadcast_to(v[i : i + 1, :], (SUB, LANES))


def from_lane(v, c):
    return jnp.broadcast_to(v[:, c : c + 1], (SUB, LANES))


def cholesky_kernel(gram_ref, upper_ref, inverse_ref, work):
    n = gram_ref.shape[0]
    tiles = n // LANES
    groups = PANEL // SUB
    sub = lax.broadcasted_iota(jnp.int32, (SUB, LANES), 0)
    lane = lax.broadcasted_iota(jnp.int32, (SUB, LANES), 1)
    row_id = lax.broadcasted_iota(jnp.int32, (n, n), 0)
    col_id = lax.broadcasted_iota(jnp.int32, (n, n), 1)
    work[:, :n] = gram_ref[...]
    work[:, n:] = jnp.where(row_id == col_id, 1.0, 0.0)
    for top in range(0, n, PANEL):
        t0 = top // LANES
        cols = list(range(t0, tiles)) + [tiles + t for t in range(t0 + 1)]
        rows_of = lambda g: slice(top + SUB * g, top + SUB * (g + 1))
        lanes_of = lambda t: slice(LANES * t, LANES * (t + 1))
        grp = [[work[rows_of(g), lanes_of(t)] for t in cols] for g in range(groups)]
        pivots = [jnp.ones((SUB, LANES), jnp.float32) for _ in range(groups)]
        for g0 in range(groups):
            c0 = (top + SUB * g0) % LANES
            heads = [[from_lane(grp[g][0], c0 + j) for j in range(SUB)] for g in range(g0, groups)]
            for i in range(SUB):
                pivot = from_row(heads[0][i], i)
                pivots[g0] = jnp.where(sub == i, pivot, pivots[g0])
                inverse = pl.reciprocal(pivot, approx=True)
                head_row = {j: from_row(heads[0][j], i) for j in range(i + 1, SUB)}
                row = [from_row(v, i) for v in grp[g0]]
                for g in range(g0, groups):
                    head = heads[g - g0]
                    factor = head[i] * inverse
                    if g == g0:
                        factor = jnp.where(sub > i, factor, 0.0)
                    for j in range(i + 1, SUB):
                        head[j] = head[j] - factor * head_row[j]
                    grp[g] = [v - factor * r for v, r in zip(grp[g], row)]
        for g in range(groups):
            scale = refine_rsqrt(pivots[g])
            for v, t in zip(grp[g], cols):
                v = v * scale
                if t < tiles:
                    v = jnp.where(lane + LANES * t >= sub + (top + SUB * g), v, 0.0)
                work[rows_of(g), lanes_of(t)] = v
        for t in range(t0):
            work[top : top + PANEL, lanes_of(t)] = jnp.zeros((PANEL, LANES), jnp.float32)
        below = top + PANEL
        if below < n:
            lo, hi = LANES * t0, n + LANES * (t0 + 1)
            first = below // LANES * LANES
            update = lax.dot_general(
                work[top:below, first:n],
                work[top:below, lo:hi],
                (((0,), (0,)), ((), ())),
                precision=HIGHEST,
                preferred_element_type=jnp.float32,
            )
            work[below:, lo:hi] = work[below:, lo:hi] - update[below - first :, :]
    upper_ref[...] = work[:, :n]
    inverse_ref[...] = work[:, n:]


def cholesky(gram):
    n = gram.shape[0]
    return pl.pallas_call(
        cholesky_kernel,
        out_shape=[jax.ShapeDtypeStruct((n, n), jnp.float32)] * 2,
        scratch_shapes=[pltpu.VMEM((n, 2 * n), jnp.float32)],
        compiler_params=pltpu.CompilerParams(vmem_limit_bytes=VMEM_LIMIT),
        cost_estimate=pl.CostEstimate(flops=2 * n * n * n, bytes_accessed=12 * n * n, transcendentals=n),
        name="cholesky256",
    )(gram)


def split(x):
    high = x.astype(jnp.bfloat16)
    return high, (x - high.astype(jnp.float32)).astype(jnp.bfloat16)


def bf16_dot(a, b):
    return jnp.dot(a, b, preferred_element_type=jnp.float32)


def core_kernel(place_ref, gram_ref, upper_ref, inverse_ref, *refs):
    blocks, (out_ref, factor_ref, high, low) = refs[:-4], refs[-4:]
    place = place_ref[0]

    @pl.when(pl.program_id(0) == 0)
    def _():
        left = upper_ref[...]
        right = rows_dot(inverse_ref[...], gram_ref[...])
        squares = jnp.sum(left * left, axis=1, keepdims=True) + jnp.sum(right * right, axis=1, keepdims=True)
        length = jnp.sqrt(squares)
        rows = jnp.concatenate([left / length, right / length], axis=1)
        factor_ref[...] = rows.T
        high[...], low[...] = split(rows)

    fh, fl = high[...], low[...]
    for s in range(0, blocks[0].shape[0], 2):
        uh, ul = split(two_slabs(place, blocks, s))
        both = bf16_dot(fh, uh) + (bf16_dot(fl, uh) + bf16_dot(fh, ul))
        out_ref[:, 0, s, :] = both[:, :LANES]
        out_ref[:, 0, s + 1, :] = both[:, LANES:]


def core_and_factor(place, gram21, upper, inverse, blocks, ny, nz):
    cells, rows, fields = blocks[0].shape
    size = rows * len(blocks)
    part = pl.BlockSpec((nz, rows, fields), lambda i: (i, 0, 0))
    return pl.pallas_call(
        core_kernel,
        grid=(ny,),
        in_specs=[pl.BlockSpec(memory_space=pltpu.SMEM)]
        + [whole((RANK, RANK))] * 3
        + [part] * len(blocks),
        out_specs=[
            pl.BlockSpec((RANK, 1, nz, fields), lambda i: (0, i, 0, 0)),
            whole((size, RANK)),
        ],
        out_shape=[
            jax.ShapeDtypeStruct((RANK, ny, nz, fields), jnp.float32),
            jax.ShapeDtypeStruct((size, RANK), jnp.float32),
        ],
        scratch_shapes=[pltpu.VMEM((RANK, size), jnp.bfloat16)] * 2,
        compiler_params=pltpu.CompilerParams(vmem_limit_bytes=VMEM_LIMIT),
        cost_estimate=pl.CostEstimate(
            flops=6 * size * RANK * cells * fields,
            bytes_accessed=4 * (size + RANK) * cells * fields,
            transcendentals=0,
        ),
        name="core",
    )(place, gram21, upper, inverse, *blocks)


def tie(x, *deps):
    return lax.optimization_barrier((x,) + deps)[0]


def block_for(snapshot, device, nz):
    rows, ny, _, fields = snapshot.shape
    cut = lax.dynamic_slice_in_dim(snapshot, device * nz, nz, axis=2)
    return cut.transpose(1, 2, 0, 3).reshape(ny * nz, rows, fields)


def on_device_blocks(snapshot, wide, narrow):
    ny, nz = snapshot.shape[1], snapshot.shape[2] // wide
    here = lax.axis_index("wide")
    place = here.astype(jnp.int32).reshape(1)
    half = wide // 2
    first = block_for(snapshot, here ^ 6, nz)
    snapshot = tie(snapshot, first)
    got = {}
    send = lambda k, *deps: over("wide", wide, k)(tie(block_for(snapshot, here ^ k, nz), *deps))
    got[6] = over("wide", wide, 6)(first)
    got[4], got[7], got[2] = send(4), send(7), send(2)
    got[5] = send(5, got[6])
    got[3] = send(3, got[2])
    got[1] = send(1, got[6])
    got[0] = block_for(snapshot, here, nz)
    blocks = [got[k] for k in range(wide)]
    own = own_gram(place, blocks[:half], ny)
    gram = full_gram(place, own, blocks, ny)
    gram = sum_over_all(gram, wide, narrow)
    upper, inverse = cholesky(gram[:RANK])
    return core_and_factor(place, gram[RANK:], upper, inverse, blocks, ny, nz)


def on_device_any(snapshot):
    regrouped = lax.all_to_all(snapshot, "wide", split_axis=2, concat_axis=0, tiled=True)
    rows_all = regrouped.shape[0]
    unfold = regrouped.reshape(rows_all, -1)
    gram = lax.dot_general(
        unfold, unfold[:RANK], (((1,), (1,)), ((), ())), precision=HIGHEST, preferred_element_type=jnp.float32
    )
    gram = lax.psum(lax.psum(gram, "narrow"), "wide")
    lower = jnp.linalg.cholesky(gram[:RANK])
    upper = jnp.concatenate(
        [lower.T, lax.linalg.triangular_solve(lower, gram[RANK:].T, left_side=True, lower=True)], axis=1
    )
    lengths = jnp.sqrt(jnp.sum(upper * upper, axis=1))
    factor = (upper / lengths[:, None]).T
    core = jnp.dot(factor.T, unfold, precision=HIGHEST, preferred_element_type=jnp.float32)
    return core.reshape((RANK,) + regrouped.shape[1:]), factor


def solution(mesh):
    wide, narrow = mesh.shape["wide"], mesh.shape["narrow"]
    if wide == FAST_WIDE:
        on_device = functools.partial(on_device_blocks, wide=wide, narrow=narrow)
    else:
        on_device = on_device_any
    return jax.shard_map(
        on_device,
        mesh=mesh,
        in_specs=(P("wide", "narrow", None, None),),
        out_specs=(P(None, "narrow", "wide", None), P()),
        check_vma=False,
    )
```

```python
import functools

import jax
import jax.numpy as jnp
from jax import lax
from jax.experimental import pallas as pl
from jax.experimental.pallas import tpu as pltpu
from jax.sharding import PartitionSpec as P

RANK = 256
LANES = 128
FAST_WIDE = 8
HIGHEST = lax.Precision.HIGHEST
VMEM_LIMIT = 16 * 1024 * 1024


def split(x):
    high = x.astype(jnp.bfloat16)
    return high, (x - high.astype(jnp.float32)).astype(jnp.bfloat16)


def by_device(place, blocks):
    distance = 1
    while distance < len(blocks):
        flag = (place & distance) != 0
        blocks = [jnp.where(flag, blocks[i ^ distance], blocks[i]) for i in range(len(blocks))]
        distance *= 2
    return blocks


def two_cells(place, refs, t):
    sides = [jnp.concatenate(by_device(place, [r[c] for r in refs]), axis=0) for c in (2 * t, 2 * t + 1)]
    return jnp.concatenate(sides, axis=1)


def rows_dot(a, b, precision=None):
    return lax.dot_general(
        a, b, (((1,), (1,)), ((), ())), precision=precision, preferred_element_type=jnp.float32
    )


def product(a, b):
    (ah, al), (bh, bl) = a, b
    left = jnp.concatenate([ah, ah, al, al], axis=1)
    right = jnp.concatenate([bh, bl, bh, bl], axis=1)
    return rows_dot(left, right)


def read(pair, t):
    return pair[0][t], pair[1][t]


def write(pair, t, value):
    pair[0][t], pair[1][t] = value


def add_to(ref, value):
    ref[...] = ref[...] + value


def start_at_zero(*refs):
    @pl.when(pl.program_id(0) == 0)
    def _():
        for ref in refs:
            ref[...] = jnp.zeros_like(ref)


def own_kernel(place_ref, *refs):
    blocks, (gram_ref, *own) = refs[:-3], refs[-3:]
    start_at_zero(gram_ref)
    for t in range(blocks[0].shape[0] // 2):
        x = split(two_cells(place_ref[0], blocks, t))
        write(own, t, x)
        add_to(gram_ref, product(x, x))


def even_kernel(place_ref, near, far, own_h, own_l, cross_ref, gram_ref, *even):
    start_at_zero(cross_ref, gram_ref)
    place = place_ref[0] // 2
    for t in range(near.shape[0] // 2):
        x = split(two_cells(place, (near, far), t))
        write(even, t, x)
        add_to(cross_ref, product(x, read((own_h, own_l), t)))
        add_to(gram_ref, product(x, x))


def odd_kernel(
    place_ref, own_gram, cross_even, gram_even, near, far, own_h, own_l, even_h, even_l,
    corner_ref, below_ref, odd_h, odd_l, all_ref,
):
    start_at_zero(all_ref)
    place = place_ref[0]
    for t in range(near.shape[0] // 2):
        x = split(two_cells(place // 2, (near, far), t))
        write((odd_h, odd_l), t, x)
        both = jnp.concatenate(x, axis=0)
        n = both.shape[0] // 2
        high = rows_dot(jnp.concatenate([own_h[t], even_h[t], x[0]], axis=0), both)
        low = rows_dot(jnp.concatenate([own_l[t], even_l[t], x[1]], axis=0), both)
        add_to(all_ref, (high[:, :n] + high[:, n:]) + (low[:, :n] + low[:, n:]))

    @pl.when(pl.program_id(0) == pl.num_programs(0) - 1)
    def _():
        n = all_ref.shape[1] // 2
        first_even = (place & 1) == 0

        def interleave(even, odd):
            a = jnp.where(first_even, even, odd)
            b = jnp.where(first_even, odd, even)
            return jnp.concatenate([a[:n], b[:n], a[n:], b[n:]], axis=0)

        low = place < FAST_WIDE // 2
        cross = interleave(cross_even[...], all_ref[:RANK].T)
        mixed = all_ref[RANK : RANK + 2 * n]
        other = interleave(
            jnp.concatenate([gram_even[...], mixed], axis=1),
            jnp.concatenate([mixed.T, all_ref[RANK + 2 * n :]], axis=1),
        ).T
        other = interleave(other[: 2 * n], other[2 * n :])
        corner = jnp.where(low, own_gram[...], other)
        corner_ref[...] = jnp.concatenate(
            [corner[:LANES, :LANES], corner[:LANES, LANES:], corner[LANES:, LANES:]], axis=0
        )
        below_ref[...] = jnp.where(low, cross, cross.T)


def whole(shape):
    return pl.BlockSpec(shape, lambda i: (0,) * len(shape))


def stepped(shape, steps):
    return pl.BlockSpec((shape[0] // steps,) + shape[1:], lambda i: (i,) + (0,) * (len(shape) - 1))


def call(kernel, name, steps, place, kept, streamed, kept_out, streamed_out, scratch=(), flops=0):
    moved = sum(4 * x.size for x in streamed) + sum(2 * s.size for s in streamed_out)
    return pl.pallas_call(
        kernel,
        grid=(steps,),
        in_specs=[pl.BlockSpec(memory_space=pltpu.SMEM)]
        + [whole(x.shape) for x in kept]
        + [stepped(x.shape, steps) for x in streamed],
        out_specs=[whole(s.shape) for s in kept_out] + [stepped(s.shape, steps) for s in streamed_out],
        out_shape=list(kept_out) + list(streamed_out),
        scratch_shapes=list(scratch),
        compiler_params=pltpu.CompilerParams(vmem_limit_bytes=VMEM_LIMIT),
        cost_estimate=pl.CostEstimate(flops=flops, bytes_accessed=moved, transcendentals=0),
        name=name,
    )(place, *kept, *streamed)


def f32(*shape):
    return jax.ShapeDtypeStruct(shape, jnp.float32)


def halves(cells, rows, fields):
    return [jax.ShapeDtypeStruct((cells // 2, rows, 2 * fields), jnp.bfloat16)] * 2


def gram_of_own(place, blocks, steps):
    cells, rows, fields = blocks[0].shape
    n = rows * len(blocks)
    return call(
        own_kernel, "own_gram", steps, place, [], blocks, [f32(n, n)], halves(cells, n, fields),
        flops=8 * n * n * cells * fields,
    )


def gram_of_even(place, near, far, own, steps):
    cells, rows, fields = near.shape
    n = 2 * rows
    return call(
        even_kernel, "even_gram", steps, place, [], [near, far, *own],
        [f32(n, 2 * n), f32(n, n)], halves(cells, n, fields), flops=24 * n * n * cells * fields,
    )


def gram_of_odd(place, kept, near, far, own, even, steps):
    cells, rows, fields = near.shape
    n = 2 * rows
    return call(
        odd_kernel, "odd_gram", steps, place, kept, [near, far, *own, *even],
        [f32(3 * LANES, LANES), f32(RANK, RANK)], halves(cells, n, fields),
        [pltpu.VMEM((4 * n, n), jnp.float32)],
        flops=32 * n * n * cells * fields,
    )


def over(axis, n, distance):
    return functools.partial(lax.ppermute, axis_name=axis, perm=[(i, i ^ distance) for i in range(n)])


def sum_over_all(x, wide, narrow):
    place = lax.axis_index("narrow")
    distances = [1 << b for b in range(narrow.bit_length() - 1)]
    for d in distances:
        side = (place & d) != 0
        n = x.shape[0] // 2
        keep = jnp.where(side, x[n:], x[:n])
        send = jnp.where(side, x[:n], x[n:])
        x = keep + over("narrow", narrow, d)(send)
    for b in range(wide.bit_length() - 1):
        x = x + over("wide", wide, 1 << b)(x)
    for d in reversed(distances):
        side = (place & d) != 0
        got = over("narrow", narrow, d)(x)
        x = jnp.where(side, jnp.concatenate([got, x]), jnp.concatenate([x, got]))
    return x


PANEL = 64
SUB = 8


def refine_rsqrt(d):
    r = lax.rsqrt(d)
    return r * (1.5 - 0.5 * d * r * r)


def from_row(v, i):
    return jnp.broadcast_to(v[i : i + 1, :], (SUB, LANES))


def from_lane(v, c):
    return jnp.broadcast_to(v[:, c : c + 1], (SUB, LANES))


def cholesky_kernel(gram_ref, upper_ref, inverse_ref, work):
    n = upper_ref.shape[0]
    tiles = n // LANES
    groups = PANEL // SUB
    sub = lax.broadcasted_iota(jnp.int32, (SUB, LANES), 0)
    lane = lax.broadcasted_iota(jnp.int32, (SUB, LANES), 1)
    row_id = lax.broadcasted_iota(jnp.int32, (n, n), 0)
    col_id = lax.broadcasted_iota(jnp.int32, (n, n), 1)
    work[:LANES, :LANES] = gram_ref[:LANES]
    work[:LANES, LANES:n] = gram_ref[LANES : 2 * LANES]
    work[LANES:, LANES:n] = gram_ref[2 * LANES :]
    work[:, n:] = jnp.where(row_id == col_id, 1.0, 0.0)
    for top in range(0, n, PANEL):
        t0 = top // LANES
        cols = list(range(t0, tiles)) + [tiles + t for t in range(t0 + 1)]
        rows_of = lambda g: slice(top + SUB * g, top + SUB * (g + 1))
        lanes_of = lambda t: slice(LANES * t, LANES * (t + 1))
        grp = [[work[rows_of(g), lanes_of(t)] for t in cols] for g in range(groups)]
        pivots = [jnp.ones((SUB, LANES), jnp.float32) for _ in range(groups)]
        for g0 in range(groups):
            c0 = (top + SUB * g0) % LANES
            heads = [[from_lane(grp[g][0], c0 + j) for j in range(SUB)] for g in range(g0, groups)]
            for i in range(SUB):
                pivot = from_row(heads[0][i], i)
                pivots[g0] = jnp.where(sub == i, pivot, pivots[g0])
                inverse = pl.reciprocal(pivot, approx=True)
                head_row = {j: from_row(heads[0][j], i) for j in range(i + 1, SUB)}
                row = [from_row(v, i) for v in grp[g0]]
                for g in range(g0, groups):
                    head = heads[g - g0]
                    factor = head[i] * inverse
                    if g == g0:
                        factor = jnp.where(sub > i, factor, 0.0)
                    for j in range(i + 1, SUB):
                        head[j] = head[j] - factor * head_row[j]
                    grp[g] = [v - factor * r for v, r in zip(grp[g], row)]
        for g in range(groups):
            scale = refine_rsqrt(pivots[g])
            for v, t in zip(grp[g], cols):
                v = v * scale
                if t < tiles:
                    v = jnp.where(lane + LANES * t >= sub + (top + SUB * g), v, 0.0)
                work[rows_of(g), lanes_of(t)] = v
        for t in range(t0):
            work[top : top + PANEL, lanes_of(t)] = jnp.zeros((PANEL, LANES), jnp.float32)
        below = top + PANEL
        if below < n:
            lo, hi = LANES * t0, n + LANES * (t0 + 1)
            first = below // LANES * LANES
            update = lax.dot_general(
                work[top:below, first:n],
                work[top:below, lo:hi],
                (((0,), (0,)), ((), ())),
                precision=HIGHEST,
                preferred_element_type=jnp.float32,
            )
            work[below:, lo:hi] = work[below:, lo:hi] - update[below - first :, :]
    upper_ref[...] = work[:, :n]
    inverse_ref[...] = work[:, n:]


def cholesky(packed):
    n = RANK
    return pl.pallas_call(
        cholesky_kernel,
        out_shape=[f32(n, n)] * 2,
        scratch_shapes=[pltpu.VMEM((n, 2 * n), jnp.float32)],
        compiler_params=pltpu.CompilerParams(vmem_limit_bytes=VMEM_LIMIT),
        cost_estimate=pl.CostEstimate(flops=2 * n * n * n, bytes_accessed=12 * n * n, transcendentals=n),
        name="cholesky256",
    )(packed)


def core_kernel(place_ref, below, upper, inverse, own_h, own_l, even_h, even_l, odd_h, odd_l, *rest):
    factor_ref, out_ref, weights = rest

    @pl.when(pl.program_id(0) == 0)
    def _():
        left = upper[...]
        right = rows_dot(inverse[...], below[...], HIGHEST)
        squares = jnp.sum(left * left, axis=1, keepdims=True) + jnp.sum(right * right, axis=1, keepdims=True)
        length = jnp.sqrt(squares)
        left, right = left / length, right / length
        factor_ref[...] = jnp.concatenate([left, right], axis=1).T
        low = place_ref[0] < 4
        own = jnp.where(low, left, right)
        other = jnp.where(low, right, left)
        n = RANK // 4
        first = jnp.concatenate([other[:, :n], other[:, 2 * n : 3 * n]], axis=1)
        second = jnp.concatenate([other[:, n : 2 * n], other[:, 3 * n :]], axis=1)
        first_even = (place_ref[0] & 1) == 0
        even = jnp.where(first_even, first, second)
        odd = jnp.where(first_even, second, first)
        high, small = split(jnp.concatenate([own, even, odd], axis=1))
        weights[...] = jnp.concatenate([high, small, high], axis=1)

    w = weights[...]
    for t in range(own_h.shape[0]):
        high = [r[t] for r in (own_h, even_h, odd_h)]
        small = [r[t] for r in (own_l, even_l, odd_l)]
        both = jnp.dot(w, jnp.concatenate(high + high + small, axis=0), preferred_element_type=jnp.float32)
        out_ref[:, 0, 2 * t, :] = both[:, :LANES]
        out_ref[:, 0, 2 * t + 1, :] = both[:, LANES:]


def core_and_factor(place, kept, streamed, ny, nz, fields):
    size = sum(x.shape[1] for x in streamed) // 2
    return pl.pallas_call(
        core_kernel,
        grid=(ny,),
        in_specs=[pl.BlockSpec(memory_space=pltpu.SMEM)]
        + [whole(x.shape) for x in kept]
        + [stepped(x.shape, ny) for x in streamed],
        out_specs=[whole((size, RANK)), pl.BlockSpec((RANK, 1, nz, fields), lambda i: (0, i, 0, 0))],
        out_shape=[f32(size, RANK), f32(RANK, ny, nz, fields)],
        scratch_shapes=[pltpu.VMEM((RANK, 3 * size), jnp.bfloat16)],
        compiler_params=pltpu.CompilerParams(vmem_limit_bytes=VMEM_LIMIT),
        cost_estimate=pl.CostEstimate(
            flops=6 * size * RANK * ny * nz * fields,
            bytes_accessed=4 * (size + RANK) * ny * nz * fields,
            transcendentals=0,
        ),
        name="core",
    )(place, *kept, *streamed)


def tie(x, *deps):
    return lax.optimization_barrier((x,) + deps)[0]


def block_for(snapshot, device, nz):
    rows, ny, _, fields = snapshot.shape
    cut = lax.dynamic_slice_in_dim(snapshot, device * nz, nz, axis=2)
    return cut.transpose(1, 2, 0, 3).reshape(ny * nz, rows, fields)


def on_device_blocks(snapshot, wide, narrow):
    ny, nz = snapshot.shape[1], snapshot.shape[2] // wide
    here = lax.axis_index("wide")
    place = here.astype(jnp.int32).reshape(1)
    first = block_for(snapshot, here ^ 6, nz)
    snapshot = tie(snapshot, first)
    got = {}
    send = lambda k, *deps: over("wide", wide, k)(tie(block_for(snapshot, here ^ k, nz), *deps))
    got[6] = over("wide", wide, 6)(first)
    got[4], got[7], got[2] = send(4), send(7), send(2)
    got[5] = send(5, got[6])
    got[3] = send(3, got[2])
    got[1] = send(1, got[6])
    got[0] = block_for(snapshot, here, nz)
    own_gram, *own = gram_of_own(place, [got[k] for k in range(4)], ny)
    cross_even, gram_even, *even = gram_of_even(place, got[4], got[6], own, ny)
    corner, below, *odd = gram_of_odd(place, [own_gram, cross_even, gram_even], got[5], got[7], own, even, ny)
    corner = sum_over_all(corner, wide, narrow)
    below = sum_over_all(below, wide, narrow)
    upper, inverse = cholesky(corner)
    factor, core = core_and_factor(
        place, [below, upper, inverse], [*own, *even, *odd], ny, nz, snapshot.shape[3]
    )
    return core, factor


def on_device_any(snapshot):
    regrouped = lax.all_to_all(snapshot, "wide", split_axis=2, concat_axis=0, tiled=True)
    rows_all = regrouped.shape[0]
    unfold = regrouped.reshape(rows_all, -1)
    gram = lax.dot_general(
        unfold, unfold[:RANK], (((1,), (1,)), ((), ())), precision=HIGHEST, preferred_element_type=jnp.float32
    )
    gram = lax.psum(lax.psum(gram, "narrow"), "wide")
    lower = jnp.linalg.cholesky(gram[:RANK])
    upper = jnp.concatenate(
        [lower.T, lax.linalg.triangular_solve(lower, gram[RANK:].T, left_side=True, lower=True)], axis=1
    )
    lengths = jnp.sqrt(jnp.sum(upper * upper, axis=1))
    factor = (upper / lengths[:, None]).T
    core = jnp.dot(factor.T, unfold, precision=HIGHEST, preferred_element_type=jnp.float32)
    return core.reshape((RANK,) + regrouped.shape[1:]), factor


def solution(mesh):
    wide, narrow = mesh.shape["wide"], mesh.shape["narrow"]
    if wide == FAST_WIDE:
        on_device = functools.partial(on_device_blocks, wide=wide, narrow=narrow)
    else:
        on_device = on_device_any
    return jax.shard_map(
        on_device,
        mesh=mesh,
        in_specs=(P("wide", "narrow", None, None),),
        out_specs=(P(None, "narrow", "wide", None), P()),
        check_vma=False,
    )
```

```python
import functools

import jax
import jax.numpy as jnp
from jax import lax
from jax.experimental import pallas as pl
from jax.experimental.pallas import tpu as pltpu
from jax.sharding import PartitionSpec as P

RANK = 256
LANES = 128
FAST_WIDE = 8
HIGHEST = lax.Precision.HIGHEST
VMEM_LIMIT = 16 * 1024 * 1024


def split(x):
    high = x.astype(jnp.bfloat16)
    return high, (x - high.astype(jnp.float32)).astype(jnp.bfloat16)


def by_device(place, blocks):
    distance = 1
    while distance < len(blocks):
        flag = (place & distance) != 0
        blocks = [jnp.where(flag, blocks[i ^ distance], blocks[i]) for i in range(len(blocks))]
        distance *= 2
    return blocks


def two_cells(place, refs, t):
    sides = [jnp.concatenate(by_device(place, [r[c] for r in refs]), axis=0) for c in (2 * t, 2 * t + 1)]
    return jnp.concatenate(sides, axis=1)


def rows_dot(a, b, precision=None):
    return lax.dot_general(
        a, b, (((1,), (1,)), ((), ())), precision=precision, preferred_element_type=jnp.float32
    )


def product(a, b):
    (ah, al), (bh, bl) = a, b
    left = jnp.concatenate([ah, ah, al, al], axis=1)
    right = jnp.concatenate([bh, bl, bh, bl], axis=1)
    return rows_dot(left, right)


def read(pair, t):
    return pair[0][t], pair[1][t]


def write(pair, t, value):
    pair[0][t], pair[1][t] = value


def add_to(ref, value):
    ref[...] = ref[...] + value


def start_at_zero(*refs):
    @pl.when(pl.program_id(0) == 0)
    def _():
        for ref in refs:
            ref[...] = jnp.zeros_like(ref)


def own_kernel(place_ref, *refs):
    blocks, (gram_ref, *own) = refs[:-3], refs[-3:]
    start_at_zero(gram_ref)
    for t in range(blocks[0].shape[0] // 2):
        x = split(two_cells(place_ref[0], blocks, t))
        write(own, t, x)
        add_to(gram_ref, product(x, x))


def even_kernel(place_ref, near, far, own_h, own_l, cross_ref, gram_ref, *even):
    start_at_zero(cross_ref, gram_ref)
    place = place_ref[0] // 2
    for t in range(near.shape[0] // 2):
        x = split(two_cells(place, (near, far), t))
        write(even, t, x)
        add_to(cross_ref, product(x, read((own_h, own_l), t)))
        add_to(gram_ref, product(x, x))


def odd_kernel(
    place_ref, own_gram, cross_even, gram_even, near, far, own_h, own_l, even_h, even_l,
    corner_ref, below_ref, odd_h, odd_l, all_ref,
):
    start_at_zero(all_ref)
    place = place_ref[0]
    for t in range(near.shape[0] // 2):
        x = split(two_cells(place // 2, (near, far), t))
        write((odd_h, odd_l), t, x)
        both = jnp.concatenate(x, axis=0)
        n = both.shape[0] // 2
        high = rows_dot(jnp.concatenate([own_h[t], even_h[t], x[0]], axis=0), both)
        low = rows_dot(jnp.concatenate([own_l[t], even_l[t], x[1]], axis=0), both)
        add_to(all_ref, (high[:, :n] + high[:, n:]) + (low[:, :n] + low[:, n:]))

    @pl.when(pl.program_id(0) == pl.num_programs(0) - 1)
    def _():
        n = all_ref.shape[1] // 2
        first_even = (place & 1) == 0

        def interleave(even, odd):
            a = jnp.where(first_even, even, odd)
            b = jnp.where(first_even, odd, even)
            return jnp.concatenate([a[:n], b[:n], a[n:], b[n:]], axis=0)

        low = place < FAST_WIDE // 2
        cross = interleave(cross_even[...], all_ref[:RANK].T)
        mixed = all_ref[RANK : RANK + 2 * n]
        other = interleave(
            jnp.concatenate([gram_even[...], mixed], axis=1),
            jnp.concatenate([mixed.T, all_ref[RANK + 2 * n :]], axis=1),
        ).T
        other = interleave(other[: 2 * n], other[2 * n :])
        corner = jnp.where(low, own_gram[...], other)
        corner_ref[...] = jnp.concatenate(
            [corner[:LANES, :LANES], corner[:LANES, LANES:], corner[LANES:, LANES:]], axis=0
        )
        below_ref[...] = jnp.where(low, cross, cross.T)


def whole(shape):
    return pl.BlockSpec(shape, lambda i: (0,) * len(shape))


def stepped(shape, steps):
    return pl.BlockSpec((shape[0] // steps,) + shape[1:], lambda i: (i,) + (0,) * (len(shape) - 1))


def call(kernel, name, steps, place, kept, streamed, kept_out, streamed_out, scratch=(), flops=0):
    moved = sum(4 * x.size for x in streamed) + sum(2 * s.size for s in streamed_out)
    return pl.pallas_call(
        kernel,
        grid=(steps,),
        in_specs=[pl.BlockSpec(memory_space=pltpu.SMEM)]
        + [whole(x.shape) for x in kept]
        + [stepped(x.shape, steps) for x in streamed],
        out_specs=[whole(s.shape) for s in kept_out] + [stepped(s.shape, steps) for s in streamed_out],
        out_shape=list(kept_out) + list(streamed_out),
        scratch_shapes=list(scratch),
        compiler_params=pltpu.CompilerParams(vmem_limit_bytes=VMEM_LIMIT),
        cost_estimate=pl.CostEstimate(flops=flops, bytes_accessed=moved, transcendentals=0),
        name=name,
    )(place, *kept, *streamed)


def f32(*shape):
    return jax.ShapeDtypeStruct(shape, jnp.float32)


def halves(cells, rows, fields):
    return [jax.ShapeDtypeStruct((cells // 2, rows, 2 * fields), jnp.bfloat16)] * 2


def gram_of_own(place, blocks, steps):
    cells, rows, fields = blocks[0].shape
    n = rows * len(blocks)
    return call(
        own_kernel, "own_gram", steps, place, [], blocks, [f32(n, n)], halves(cells, n, fields),
        flops=8 * n * n * cells * fields,
    )


def gram_of_even(place, near, far, own, steps):
    cells, rows, fields = near.shape
    n = 2 * rows
    return call(
        even_kernel, "even_gram", steps, place, [], [near, far, *own],
        [f32(n, 2 * n), f32(n, n)], halves(cells, n, fields), flops=24 * n * n * cells * fields,
    )


def gram_of_odd(place, kept, near, far, own, even, steps):
    cells, rows, fields = near.shape
    n = 2 * rows
    return call(
        odd_kernel, "odd_gram", steps, place, kept, [near, far, *own, *even],
        [f32(3 * LANES, LANES), f32(RANK, RANK)], halves(cells, n, fields),
        [pltpu.VMEM((4 * n, n), jnp.float32)],
        flops=32 * n * n * cells * fields,
    )


def over(axis, n, distance):
    return functools.partial(lax.ppermute, axis_name=axis, perm=[(i, i ^ distance) for i in range(n)])


def sum_over_all(x, wide, narrow):
    place = lax.axis_index("narrow")
    distances = [1 << b for b in range(narrow.bit_length() - 1)]
    for d in distances:
        side = (place & d) != 0
        n = x.shape[0] // 2
        keep = jnp.where(side, x[n:], x[:n])
        send = jnp.where(side, x[:n], x[n:])
        x = keep + over("narrow", narrow, d)(send)
    for b in range(wide.bit_length() - 1):
        x = x + over("wide", wide, 1 << b)(x)
    for d in reversed(distances):
        side = (place & d) != 0
        got = over("narrow", narrow, d)(x)
        x = jnp.where(side, jnp.concatenate([got, x]), jnp.concatenate([x, got]))
    return x


PANEL = 64
SUB = 8


def refine_rsqrt(d):
    r = lax.rsqrt(d)
    return r * (1.5 - 0.5 * d * r * r)


def from_row(v, i):
    return jnp.broadcast_to(v[i : i + 1, :], (SUB, LANES))


def from_lane(v, c):
    return jnp.broadcast_to(v[:, c : c + 1], (SUB, LANES))


def cholesky_kernel(gram_ref, upper_ref, inverse_ref, work):
    n = upper_ref.shape[0]
    tiles = n // LANES
    groups = PANEL // SUB
    sub = lax.broadcasted_iota(jnp.int32, (SUB, LANES), 0)
    lane = lax.broadcasted_iota(jnp.int32, (SUB, LANES), 1)
    row_id = lax.broadcasted_iota(jnp.int32, (n, n), 0)
    col_id = lax.broadcasted_iota(jnp.int32, (n, n), 1)
    work[:LANES, :LANES] = gram_ref[:LANES]
    work[:LANES, LANES:n] = gram_ref[LANES : 2 * LANES]
    work[LANES:, LANES:n] = gram_ref[2 * LANES :]
    work[:, n:] = jnp.where(row_id == col_id, 1.0, 0.0)
    for top in range(0, n, PANEL):
        t0 = top // LANES
        cols = list(range(t0, tiles)) + [tiles + t for t in range(t0 + 1)]
        rows_of = lambda g: slice(top + SUB * g, top + SUB * (g + 1))
        lanes_of = lambda t: slice(LANES * t, LANES * (t + 1))
        grp = [[work[rows_of(g), lanes_of(t)] for t in cols] for g in range(groups)]
        pivots = [jnp.ones((SUB, LANES), jnp.float32) for _ in range(groups)]
        for g0 in range(groups):
            c0 = (top + SUB * g0) % LANES
            heads = [[from_lane(grp[g][0], c0 + j) for j in range(SUB)] for g in range(g0, groups)]
            for i in range(SUB):
                pivot = from_row(heads[0][i], i)
                pivots[g0] = jnp.where(sub == i, pivot, pivots[g0])
                inverse = pl.reciprocal(pivot, approx=True)
                head_row = {j: from_row(heads[0][j], i) for j in range(i + 1, SUB)}
                row = [from_row(v, i) for v in grp[g0]]
                for g in range(g0, groups):
                    head = heads[g - g0]
                    factor = head[i] * inverse
                    if g == g0:
                        factor = jnp.where(sub > i, factor, 0.0)
                    for j in range(i + 1, SUB):
                        head[j] = head[j] - factor * head_row[j]
                    grp[g] = [v - factor * r for v, r in zip(grp[g], row)]
        for g in range(groups):
            scale = refine_rsqrt(pivots[g])
            for v, t in zip(grp[g], cols):
                v = v * scale
                if t < tiles:
                    v = jnp.where(lane + LANES * t >= sub + (top + SUB * g), v, 0.0)
                work[rows_of(g), lanes_of(t)] = v
        for t in range(t0):
            work[top : top + PANEL, lanes_of(t)] = jnp.zeros((PANEL, LANES), jnp.float32)
        below = top + PANEL
        if below < n:
            lo, hi = LANES * t0, n + LANES * (t0 + 1)
            first = below // LANES * LANES
            update = lax.dot_general(
                work[top:below, first:n],
                work[top:below, lo:hi],
                (((0,), (0,)), ((), ())),
                precision=HIGHEST,
                preferred_element_type=jnp.float32,
            )
            work[below:, lo:hi] = work[below:, lo:hi] - update[below - first :, :]
    upper_ref[...] = work[:, :n]
    inverse_ref[...] = work[:, n:]


def cholesky(packed):
    n = RANK
    return pl.pallas_call(
        cholesky_kernel,
        out_shape=[f32(n, n)] * 2,
        scratch_shapes=[pltpu.VMEM((n, 2 * n), jnp.float32)],
        compiler_params=pltpu.CompilerParams(vmem_limit_bytes=VMEM_LIMIT),
        cost_estimate=pl.CostEstimate(flops=2 * n * n * n, bytes_accessed=12 * n * n, transcendentals=n),
        name="cholesky256",
    )(packed)


def core_kernel(place_ref, below, upper, inverse, own_h, own_l, even_h, even_l, odd_h, odd_l, *rest):
    factor_ref, out_ref, weights = rest

    @pl.when(pl.program_id(0) == 0)
    def _():
        left = upper[...]
        right = rows_dot(inverse[...], below[...], HIGHEST)
        squares = jnp.sum(left * left, axis=1, keepdims=True) + jnp.sum(right * right, axis=1, keepdims=True)
        length = jnp.sqrt(squares)
        left, right = left / length, right / length
        factor_ref[...] = jnp.concatenate([left, right], axis=1).T
        low = place_ref[0] < 4
        own = jnp.where(low, left, right)
        other = jnp.where(low, right, left)
        n = RANK // 4
        first = jnp.concatenate([other[:, :n], other[:, 2 * n : 3 * n]], axis=1)
        second = jnp.concatenate([other[:, n : 2 * n], other[:, 3 * n :]], axis=1)
        first_even = (place_ref[0] & 1) == 0
        even = jnp.where(first_even, first, second)
        odd = jnp.where(first_even, second, first)
        high, small = split(jnp.concatenate([own, even, odd], axis=1))
        weights[...] = jnp.concatenate([high, small, high], axis=1)

    w = weights[...]
    for t in range(own_h.shape[0]):
        high = [r[t] for r in (own_h, even_h, odd_h)]
        small = [r[t] for r in (own_l, even_l, odd_l)]
        both = jnp.dot(w, jnp.concatenate(high + high + small, axis=0), preferred_element_type=jnp.float32)
        out_ref[:, 0, 2 * t, :] = both[:, :LANES]
        out_ref[:, 0, 2 * t + 1, :] = both[:, LANES:]


def core_and_factor(place, kept, streamed, ny, nz, fields):
    size = sum(x.shape[1] for x in streamed) // 2
    return pl.pallas_call(
        core_kernel,
        grid=(ny,),
        in_specs=[pl.BlockSpec(memory_space=pltpu.SMEM)]
        + [whole(x.shape) for x in kept]
        + [stepped(x.shape, ny) for x in streamed],
        out_specs=[whole((size, RANK)), pl.BlockSpec((RANK, 1, nz, fields), lambda i: (0, i, 0, 0))],
        out_shape=[f32(size, RANK), f32(RANK, ny, nz, fields)],
        scratch_shapes=[pltpu.VMEM((RANK, 3 * size), jnp.bfloat16)],
        compiler_params=pltpu.CompilerParams(vmem_limit_bytes=VMEM_LIMIT),
        cost_estimate=pl.CostEstimate(
            flops=6 * size * RANK * ny * nz * fields,
            bytes_accessed=4 * (size + RANK) * ny * nz * fields,
            transcendentals=0,
        ),
        name="core",
    )(place, *kept, *streamed)


def tie(x, *deps):
    return lax.optimization_barrier((x,) + deps)[0]


def block_for(snapshot, device, nz):
    rows, ny, _, fields = snapshot.shape
    cut = lax.dynamic_slice_in_dim(snapshot, device * nz, nz, axis=2)
    return cut.transpose(1, 2, 0, 3).reshape(ny * nz, rows, fields)


def on_device_blocks(snapshot, wide, narrow):
    ny, nz = snapshot.shape[1], snapshot.shape[2] // wide
    here = lax.axis_index("wide")
    place = here.astype(jnp.int32).reshape(1)
    first = block_for(snapshot, here ^ 6, nz)
    snapshot = tie(snapshot, first)
    got = {}
    send = lambda k, *deps: over("wide", wide, k)(tie(block_for(snapshot, here ^ k, nz), *deps))
    got[6] = over("wide", wide, 6)(first)
    got[4], got[2], got[1] = send(4), send(2), send(1)
    got[3] = send(3, got[6])
    got[5] = send(5, got[6])
    got[7] = send(7, got[4])
    got[0] = block_for(snapshot, here, nz)
    own_gram, *own = gram_of_own(place, [got[k] for k in range(4)], ny)
    cross_even, gram_even, *even = gram_of_even(place, got[4], got[6], own, ny)
    corner, below, *odd = gram_of_odd(place, [own_gram, cross_even, gram_even], got[5], got[7], own, even, ny)
    corner = sum_over_all(corner, wide, narrow)
    below = sum_over_all(below, wide, narrow)
    upper, inverse = cholesky(corner)
    factor, core = core_and_factor(
        place, [below, upper, inverse], [*own, *even, *odd], ny, nz, snapshot.shape[3]
    )
    return core, factor


def on_device_any(snapshot):
    regrouped = lax.all_to_all(snapshot, "wide", split_axis=2, concat_axis=0, tiled=True)
    rows_all = regrouped.shape[0]
    unfold = regrouped.reshape(rows_all, -1)
    gram = lax.dot_general(
        unfold, unfold[:RANK], (((1,), (1,)), ((), ())), precision=HIGHEST, preferred_element_type=jnp.float32
    )
    gram = lax.psum(lax.psum(gram, "narrow"), "wide")
    lower = jnp.linalg.cholesky(gram[:RANK])
    upper = jnp.concatenate(
        [lower.T, lax.linalg.triangular_solve(lower, gram[RANK:].T, left_side=True, lower=True)], axis=1
    )
    lengths = jnp.sqrt(jnp.sum(upper * upper, axis=1))
    factor = (upper / lengths[:, None]).T
    core = jnp.dot(factor.T, unfold, precision=HIGHEST, preferred_element_type=jnp.float32)
    return core.reshape((RANK,) + regrouped.shape[1:]), factor


def solution(mesh):
    wide, narrow = mesh.shape["wide"], mesh.shape["narrow"]
    if wide == FAST_WIDE:
        on_device = functools.partial(on_device_blocks, wide=wide, narrow=narrow)
    else:
        on_device = on_device_any
    return jax.shard_map(
        on_device,
        mesh=mesh,
        in_specs=(P("wide", "narrow", None, None),),
        out_specs=(P(None, "narrow", "wide", None), P()),
        check_vma=False,
    )
```

```python
import functools

import jax
import jax.numpy as jnp
from jax import lax
from jax.experimental import pallas as pl
from jax.experimental.pallas import tpu as pltpu
from jax.sharding import PartitionSpec as P

RANK = 256
LANES = 128
FAST_WIDE, FAST_NARROW = 8, 4
LATE = 1
LATE_STEPS = 2
HIGHEST = lax.Precision.HIGHEST
VMEM_LIMIT = 16 * 1024 * 1024


def split(x):
    high = x.astype(jnp.bfloat16)
    return high, (x - high.astype(jnp.float32)).astype(jnp.bfloat16)


def by_device(place, blocks):
    distance = 1
    while distance < len(blocks):
        flag = (place & distance) != 0
        blocks = [jnp.where(flag, blocks[i ^ distance], blocks[i]) for i in range(len(blocks))]
        distance *= 2
    return blocks


def two_cells(place, refs, t):
    sides = [jnp.concatenate(by_device(place, [r[c] for r in refs]), axis=0) for c in (2 * t, 2 * t + 1)]
    return jnp.concatenate(sides, axis=1)


def rows_dot(a, b, precision=None):
    return lax.dot_general(
        a, b, (((1,), (1,)), ((), ())), precision=precision, preferred_element_type=jnp.float32
    )


def product(a, b):
    (ah, al), (bh, bl) = a, b
    left = jnp.concatenate([ah, ah, al, al], axis=1)
    right = jnp.concatenate([bh, bl, bh, bl], axis=1)
    return rows_dot(left, right)


def read(pair, t):
    return pair[0][t], pair[1][t]


def write(pair, t, value):
    pair[0][t], pair[1][t] = value


def add_to(ref, value):
    ref[...] = ref[...] + value


def start_at_zero(*refs):
    @pl.when(pl.program_id(0) == 0)
    def _():
        for ref in refs:
            ref[...] = jnp.zeros_like(ref)


def own_kernel(place_ref, *refs):
    blocks, (gram_ref, *own) = refs[:-3], refs[-3:]
    start_at_zero(gram_ref)
    for t in range(blocks[0].shape[0] // 2):
        x = split(two_cells(place_ref[0], blocks, t))
        write(own, t, x)
        add_to(gram_ref, product(x, x))


def even_kernel(place_ref, near, far, own_h, own_l, cross_ref, gram_ref, *even):
    start_at_zero(cross_ref, gram_ref)
    place = place_ref[0] // 2
    for t in range(near.shape[0] // 2):
        x = split(two_cells(place, (near, far), t))
        write(even, t, x)
        add_to(cross_ref, product(x, read((own_h, own_l), t)))
        add_to(gram_ref, product(x, x))


def add_odd(place_ref, near, far, own, even, odd, all_ref):
    for t in range(near.shape[0] // 2):
        x = split(two_cells(place_ref[0] // 2, (near, far), t))
        write(odd, t, x)
        both = jnp.concatenate(x, axis=0)
        n = both.shape[0] // 2
        high = rows_dot(jnp.concatenate([own[0][t], even[0][t], x[0]], axis=0), both)
        low = rows_dot(jnp.concatenate([own[1][t], even[1][t], x[1]], axis=0), both)
        add_to(all_ref, (high[:, :n] + high[:, n:]) + (low[:, :n] + low[:, n:]))


def odd_kernel(place_ref, near, far, own_h, own_l, even_h, even_l, all_ref, odd_h, odd_l):
    start_at_zero(all_ref)
    add_odd(place_ref, near, far, (own_h, own_l), (even_h, even_l), (odd_h, odd_l), all_ref)


def last_kernel(
    place_ref, own_gram, cross_even, gram_even, all_odd, near, far, own_h, own_l, even_h, even_l, _, __,
    corner_ref, below_ref, odd_h, odd_l, all_ref,
):
    @pl.when(pl.program_id(0) == 0)
    def _():
        all_ref[...] = all_odd[...]

    add_odd(place_ref, near, far, (own_h, own_l), (even_h, even_l), (odd_h, odd_l), all_ref)
    place = place_ref[0]

    @pl.when(pl.program_id(0) == pl.num_programs(0) - 1)
    def _():
        n = all_ref.shape[1] // 2
        first_even = (place & 1) == 0

        def interleave(even, odd):
            a = jnp.where(first_even, even, odd)
            b = jnp.where(first_even, odd, even)
            return jnp.concatenate([a[:n], b[:n], a[n:], b[n:]], axis=0)

        low = place < FAST_WIDE // 2
        cross = interleave(cross_even[...], all_ref[:RANK].T)
        mixed = all_ref[RANK : RANK + 2 * n]
        other = interleave(
            jnp.concatenate([gram_even[...], mixed], axis=1),
            jnp.concatenate([mixed.T, all_ref[RANK + 2 * n :]], axis=1),
        ).T
        other = interleave(other[: 2 * n], other[2 * n :])
        corner = jnp.where(low, own_gram[...], other)
        corner_ref[...] = jnp.concatenate(
            [corner[:LANES, :LANES], corner[:LANES, LANES:], corner[LANES:, LANES:]], axis=0
        )
        below_ref[...] = jnp.where(low, cross, cross.T)


def whole(shape):
    return pl.BlockSpec(shape, lambda i: (0,) * len(shape))


def parts_of(x, size, first=0):
    return pl.BlockSpec((size,) + x.shape[1:], lambda i: (i + first,) + (0,) * (len(x.shape) - 1))


def call(
    kernel, name, steps, place, kept, blocks, split_blocks, kept_out, out, first=0, filled=(), scratch=(), flops=0
):
    pairs = blocks[0].shape[0] // 2 // steps
    moved = sum(4 * x.size for x in blocks) + sum(2 * s.size for s in out)
    return pl.pallas_call(
        kernel,
        grid=(steps,),
        in_specs=[pl.BlockSpec(memory_space=pltpu.SMEM)]
        + [whole(x.shape) for x in kept]
        + [parts_of(x, 2 * pairs) for x in blocks]
        + [parts_of(x, pairs, first) for x in split_blocks]
        + [pl.BlockSpec(memory_space=pl.ANY) for _ in filled],
        out_specs=[whole(s.shape) for s in kept_out] + [parts_of(s, pairs, first) for s in out],
        out_shape=list(kept_out) + list(out),
        scratch_shapes=list(scratch),
        input_output_aliases={
            1 + len(kept) + len(blocks) + len(split_blocks) + i: len(kept_out) + i for i in range(len(filled))
        },
        compiler_params=pltpu.CompilerParams(vmem_limit_bytes=VMEM_LIMIT),
        cost_estimate=pl.CostEstimate(flops=flops, bytes_accessed=moved, transcendentals=0),
        name=name,
    )(place, *kept, *blocks, *split_blocks, *filled)


def f32(*shape):
    return jax.ShapeDtypeStruct(shape, jnp.float32)


def halves(cells, rows, fields):
    return [jax.ShapeDtypeStruct((cells // 2, rows, 2 * fields), jnp.bfloat16)] * 2


def gram_of_own(place, blocks, steps):
    cells, rows, fields = blocks[0].shape
    n = rows * len(blocks)
    return call(
        own_kernel, "own_gram", steps, place, [], blocks, [], [f32(n, n)], halves(cells, n, fields),
        flops=8 * n * n * cells * fields,
    )


def gram_of_even(place, near, far, own, steps):
    cells, rows, fields = near.shape
    n = 2 * rows
    return call(
        even_kernel, "even_gram", steps, place, [], [near, far], own,
        [f32(n, 2 * n), f32(n, n)], halves(cells, n, fields), flops=24 * n * n * cells * fields,
    )


def gram_of_odd(place, near, far, own, even, steps):
    cells, rows, fields = near.shape
    n = 2 * rows
    return call(
        odd_kernel, "odd_gram", steps, place, [], [near, far], [*own, *even],
        [f32(4 * n, n)], halves(2 * own[0].shape[0], n, fields), flops=32 * n * n * cells * fields,
    )


def gram_of_last(place, kept, near, far, own, even, odd, steps):
    cells, rows, fields = near.shape
    n = 2 * rows
    pairs = cells // 2 // steps
    return call(
        last_kernel, "last_gram", steps, place, kept, [near, far], [*own, *even],
        [f32(3 * LANES, LANES), f32(RANK, RANK)], halves(2 * own[0].shape[0], n, fields), own[0].shape[0] // pairs - steps, odd,
        [pltpu.VMEM((4 * n, n), jnp.float32)], flops=32 * n * n * cells * fields,
    )


def over(step):
    axis, n, distance = step
    return functools.partial(lax.ppermute, axis_name=axis, perm=[(i, i ^ distance) for i in range(n)])


def sum_over_all(x, halved, doubled):
    sides = [(lax.axis_index(axis) & distance) != 0 for axis, _, distance in halved]
    for step, side in zip(halved, sides):
        n = x.shape[0] // 2
        keep = jnp.where(side, x[n:], x[:n])
        send = jnp.where(side, x[:n], x[n:])
        x = keep + over(step)(send)
    for step in doubled:
        x = x + over(step)(x)
    for step, side in reversed(list(zip(halved, sides))):
        got = over(step)(x)
        x = jnp.where(side, jnp.concatenate([got, x]), jnp.concatenate([x, got]))
    return x


def sum_both(corner, below, wide, narrow):
    core, y = ("narrow", narrow, 1), ("narrow", narrow, 2)
    x, z_near, z_far = [("wide", wide, 1 << b) for b in range(3)]
    corner = sum_over_all(corner, [core, y], [z_far, x, z_near])
    below = sum_over_all(below, [core, x], [y, z_near, z_far])
    return corner, below


PANEL = 64
SUB = 8


def refine_rsqrt(d):
    r = lax.rsqrt(d)
    return r * (1.5 - 0.5 * d * r * r)


def from_row(v, i):
    return jnp.broadcast_to(v[i : i + 1, :], (SUB, LANES))


def from_lane(v, c):
    return jnp.broadcast_to(v[:, c : c + 1], (SUB, LANES))


def cholesky_kernel(gram_ref, upper_ref, inverse_ref, work):
    n = upper_ref.shape[0]
    tiles = n // LANES
    groups = PANEL // SUB
    sub = lax.broadcasted_iota(jnp.int32, (SUB, LANES), 0)
    lane = lax.broadcasted_iota(jnp.int32, (SUB, LANES), 1)
    row_id = lax.broadcasted_iota(jnp.int32, (n, n), 0)
    col_id = lax.broadcasted_iota(jnp.int32, (n, n), 1)
    work[:LANES, :LANES] = gram_ref[:LANES]
    work[:LANES, LANES:n] = gram_ref[LANES : 2 * LANES]
    work[LANES:, LANES:n] = gram_ref[2 * LANES :]
    work[:, n:] = jnp.where(row_id == col_id, 1.0, 0.0)
    for top in range(0, n, PANEL):
        t0 = top // LANES
        cols = list(range(t0, tiles)) + [tiles + t for t in range(t0 + 1)]
        rows_of = lambda g: slice(top + SUB * g, top + SUB * (g + 1))
        lanes_of = lambda t: slice(LANES * t, LANES * (t + 1))
        grp = [[work[rows_of(g), lanes_of(t)] for t in cols] for g in range(groups)]
        pivots = [jnp.ones((SUB, LANES), jnp.float32) for _ in range(groups)]
        for g0 in range(groups):
            c0 = (top + SUB * g0) % LANES
            heads = [[from_lane(grp[g][0], c0 + j) for j in range(SUB)] for g in range(g0, groups)]
            for i in range(SUB):
                pivot = from_row(heads[0][i], i)
                pivots[g0] = jnp.where(sub == i, pivot, pivots[g0])
                inverse = pl.reciprocal(pivot, approx=True)
                head_row = {j: from_row(heads[0][j], i) for j in range(i + 1, SUB)}
                row = [from_row(v, i) for v in grp[g0]]
                for g in range(g0, groups):
                    head = heads[g - g0]
                    factor = head[i] * inverse
                    if g == g0:
                        factor = jnp.where(sub > i, factor, 0.0)
                    for j in range(i + 1, SUB):
                        head[j] = head[j] - factor * head_row[j]
                    grp[g] = [v - factor * r for v, r in zip(grp[g], row)]
        for g in range(groups):
            scale = refine_rsqrt(pivots[g])
            for v, t in zip(grp[g], cols):
                v = v * scale
                if t < tiles:
                    v = jnp.where(lane + LANES * t >= sub + (top + SUB * g), v, 0.0)
                work[rows_of(g), lanes_of(t)] = v
        for t in range(t0):
            work[top : top + PANEL, lanes_of(t)] = jnp.zeros((PANEL, LANES), jnp.float32)
        below = top + PANEL
        if below < n:
            lo, hi = LANES * t0, n + LANES * (t0 + 1)
            first = below // LANES * LANES
            update = lax.dot_general(
                work[top:below, first:n],
                work[top:below, lo:hi],
                (((0,), (0,)), ((), ())),
                precision=HIGHEST,
                preferred_element_type=jnp.float32,
            )
            work[below:, lo:hi] = work[below:, lo:hi] - update[below - first :, :]
    upper_ref[...] = work[:, :n]
    inverse_ref[...] = work[:, n:]


def cholesky(packed):
    n = RANK
    return pl.pallas_call(
        cholesky_kernel,
        out_shape=[f32(n, n)] * 2,
        scratch_shapes=[pltpu.VMEM((n, 2 * n), jnp.float32)],
        compiler_params=pltpu.CompilerParams(vmem_limit_bytes=VMEM_LIMIT),
        cost_estimate=pl.CostEstimate(flops=2 * n * n * n, bytes_accessed=12 * n * n, transcendentals=n),
        name="cholesky256",
    )(packed)


def core_kernel(place_ref, below, upper, inverse, own_h, own_l, even_h, even_l, odd_h, odd_l, *rest):
    factor_ref, out_ref, weights = rest

    @pl.when(pl.program_id(0) == 0)
    def _():
        left = upper[...]
        right = rows_dot(inverse[...], below[...], HIGHEST)
        squares = jnp.sum(left * left, axis=1, keepdims=True) + jnp.sum(right * right, axis=1, keepdims=True)
        length = jnp.sqrt(squares)
        left, right = left / length, right / length
        factor_ref[...] = jnp.concatenate([left, right], axis=1).T
        low = place_ref[0] < 4
        own = jnp.where(low, left, right)
        other = jnp.where(low, right, left)
        n = RANK // 4
        first = jnp.concatenate([other[:, :n], other[:, 2 * n : 3 * n]], axis=1)
        second = jnp.concatenate([other[:, n : 2 * n], other[:, 3 * n :]], axis=1)
        first_even = (place_ref[0] & 1) == 0
        even = jnp.where(first_even, first, second)
        odd = jnp.where(first_even, second, first)
        high, small = split(jnp.concatenate([own, even, odd], axis=1))
        weights[...] = jnp.concatenate([high, small, high], axis=1)

    w = weights[...]
    for t in range(own_h.shape[0]):
        high = [r[t] for r in (own_h, even_h, odd_h)]
        small = [r[t] for r in (own_l, even_l, odd_l)]
        both = jnp.dot(w, jnp.concatenate(high + high + small, axis=0), preferred_element_type=jnp.float32)
        out_ref[:, 0, 2 * t, :] = both[:, :LANES]
        out_ref[:, 0, 2 * t + 1, :] = both[:, LANES:]


def core_and_factor(place, kept, streamed, ny, nz, fields):
    size = sum(x.shape[1] for x in streamed) // 2
    return pl.pallas_call(
        core_kernel,
        grid=(ny,),
        in_specs=[pl.BlockSpec(memory_space=pltpu.SMEM)]
        + [whole(x.shape) for x in kept]
        + [parts_of(x, nz // 2) for x in streamed],
        out_specs=[whole((size, RANK)), pl.BlockSpec((RANK, 1, nz, fields), lambda i: (0, i, 0, 0))],
        out_shape=[f32(size, RANK), f32(RANK, ny, nz, fields)],
        scratch_shapes=[pltpu.VMEM((RANK, 3 * size), jnp.bfloat16)],
        compiler_params=pltpu.CompilerParams(vmem_limit_bytes=VMEM_LIMIT),
        cost_estimate=pl.CostEstimate(
            flops=6 * size * RANK * ny * nz * fields,
            bytes_accessed=4 * (size + RANK) * ny * nz * fields,
            transcendentals=0,
        ),
        name="core",
    )(place, *kept, *streamed)


def tie(x, *deps):
    return lax.optimization_barrier((x,) + deps)[0]


def block_for(snapshot, device, nz):
    rows, ny, _, fields = snapshot.shape
    cut = lax.dynamic_slice_in_dim(snapshot, device * nz, nz, axis=2)
    return cut.transpose(1, 2, 0, 3).reshape(ny * nz, rows, fields)


def on_device_blocks(snapshot, wide, narrow):
    ny, nz = snapshot.shape[1], snapshot.shape[2] // wide
    here = lax.axis_index("wide")
    place = here.astype(jnp.int32).reshape(1)
    first = block_for(snapshot, here ^ 6, nz)
    snapshot = tie(snapshot, first)
    got = {}
    send = lambda k, *deps: over(("wide", wide, k))(tie(block_for(snapshot, here ^ k, nz), *deps))
    got[6] = over(("wide", wide, 6))(first)
    got[4], got[2], got[1] = send(4), send(2), send(1)
    got[3] = send(3, got[6])
    split_at = (ny - LATE) * nz
    blocks, late = {}, {}
    for k, after in ((5, 6), (7, 4)):
        block = tie(block_for(snapshot, here ^ k, nz), got[after])
        got[k] = over(("wide", wide, k))(block[:split_at])
        blocks[k] = block[split_at:]
    late[5] = over(("wide", wide, 5))(tie(blocks[5], got[7]))
    late[7] = over(("wide", wide, 7))(tie(blocks[7], got[7]))
    got[0] = block_for(snapshot, here, nz)
    own_gram, *own = gram_of_own(place, [got[k] for k in range(4)], ny)
    cross_even, gram_even, *even = gram_of_even(place, got[4], got[6], own, ny)
    all_odd, *odd = gram_of_odd(place, got[5], got[7], own, even, ny - LATE)
    kept = [own_gram, cross_even, gram_even, all_odd]
    corner, below, *odd = gram_of_last(place, kept, late[5], late[7], own, even, odd, LATE * LATE_STEPS)
    corner, below = sum_both(corner, below, wide, narrow)
    upper, inverse = cholesky(corner)
    factor, core = core_and_factor(
        place, [below, upper, inverse], [*own, *even, *odd], ny, nz, snapshot.shape[3]
    )
    return core, factor


def on_device_any(snapshot):
    regrouped = lax.all_to_all(snapshot, "wide", split_axis=2, concat_axis=0, tiled=True)
    rows_all = regrouped.shape[0]
    unfold = regrouped.reshape(rows_all, -1)
    gram = lax.dot_general(
        unfold, unfold[:RANK], (((1,), (1,)), ((), ())), precision=HIGHEST, preferred_element_type=jnp.float32
    )
    gram = lax.psum(lax.psum(gram, "narrow"), "wide")
    lower = jnp.linalg.cholesky(gram[:RANK])
    upper = jnp.concatenate(
        [lower.T, lax.linalg.triangular_solve(lower, gram[RANK:].T, left_side=True, lower=True)], axis=1
    )
    lengths = jnp.sqrt(jnp.sum(upper * upper, axis=1))
    factor = (upper / lengths[:, None]).T
    core = jnp.dot(factor.T, unfold, precision=HIGHEST, preferred_element_type=jnp.float32)
    return core.reshape((RANK,) + regrouped.shape[1:]), factor


def solution(mesh):
    wide, narrow = mesh.shape["wide"], mesh.shape["narrow"]
    if (wide, narrow) == (FAST_WIDE, FAST_NARROW):
        on_device = functools.partial(on_device_blocks, wide=wide, narrow=narrow)
    else:
        on_device = on_device_any
    return jax.shard_map(
        on_device,
        mesh=mesh,
        in_specs=(P("wide", "narrow", None, None),),
        out_specs=(P(None, "narrow", "wide", None), P()),
        check_vma=False,
    )
```

```python
import functools

import jax
import jax.numpy as jnp
from jax import lax
from jax.experimental import pallas as pl
from jax.experimental.pallas import tpu as pltpu
from jax.sharding import PartitionSpec as P

RANK = 256
LANES = 128
FAST_WIDE, FAST_NARROW = 8, 4
LATE = 1
LATE_STEPS = 2
HIGHEST = lax.Precision.HIGHEST
VMEM_LIMIT = 16 * 1024 * 1024


def split_off(x):
    high = x.astype(jnp.bfloat16)
    return high, x - high.astype(jnp.float32)


def split(x):
    high, rest = split_off(x)
    return high, rest.astype(jnp.bfloat16)


def by_device(place, blocks):
    distance = 1
    while distance < len(blocks):
        flag = (place & distance) != 0
        blocks = [jnp.where(flag, blocks[i ^ distance], blocks[i]) for i in range(len(blocks))]
        distance *= 2
    return blocks


def two_cells(place, refs, t):
    sides = [jnp.concatenate(by_device(place, [r[c] for r in refs]), axis=0) for c in (2 * t, 2 * t + 1)]
    return jnp.concatenate(sides, axis=1)


def rows_dot(a, b, precision=None):
    return lax.dot_general(
        a, b, (((1,), (1,)), ((), ())), precision=precision, preferred_element_type=jnp.float32
    )


def product(a, b):
    (ah, al), (bh, bl) = a, b
    left = jnp.concatenate([ah, ah, al, al], axis=1)
    right = jnp.concatenate([bh, bl, bh, bl], axis=1)
    return rows_dot(left, right)


def read(pair, t):
    return pair[0][t], pair[1][t]


def write(pair, t, value):
    pair[0][t], pair[1][t] = value


def add_to(ref, value):
    ref[...] = ref[...] + value


def start_at_zero(*refs):
    @pl.when(pl.program_id(0) == 0)
    def _():
        for ref in refs:
            ref[...] = jnp.zeros_like(ref)


def own_kernel(place_ref, *refs):
    blocks, (gram_ref, *own) = refs[:-3], refs[-3:]
    start_at_zero(gram_ref)
    for t in range(blocks[0].shape[0] // 2):
        x = split(two_cells(place_ref[0], blocks, t))
        write(own, t, x)
        add_to(gram_ref, product(x, x))


def even_kernel(place_ref, near, far, own_h, own_l, cross_ref, gram_ref, *even):
    start_at_zero(cross_ref, gram_ref)
    place = place_ref[0] // 2
    for t in range(near.shape[0] // 2):
        x = split(two_cells(place, (near, far), t))
        write(even, t, x)
        add_to(cross_ref, product(x, read((own_h, own_l), t)))
        add_to(gram_ref, product(x, x))


def add_odd(place_ref, near, far, own, even, odd, all_ref):
    for t in range(near.shape[0] // 2):
        x = split(two_cells(place_ref[0] // 2, (near, far), t))
        write(odd, t, x)
        both = jnp.concatenate(x, axis=0)
        n = both.shape[0] // 2
        high = rows_dot(jnp.concatenate([own[0][t], even[0][t], x[0]], axis=0), both)
        low = rows_dot(jnp.concatenate([own[1][t], even[1][t], x[1]], axis=0), both)
        add_to(all_ref, (high[:, :n] + high[:, n:]) + (low[:, :n] + low[:, n:]))


def odd_kernel(place_ref, near, far, own_h, own_l, even_h, even_l, all_ref, odd_h, odd_l):
    start_at_zero(all_ref)
    add_odd(place_ref, near, far, (own_h, own_l), (even_h, even_l), (odd_h, odd_l), all_ref)


def last_kernel(
    place_ref, own_gram, cross_even, gram_even, all_odd, near, far, own_h, own_l, even_h, even_l, _, __,
    corner_ref, below_ref, odd_h, odd_l, all_ref,
):
    @pl.when(pl.program_id(0) == 0)
    def _():
        all_ref[...] = all_odd[...]

    add_odd(place_ref, near, far, (own_h, own_l), (even_h, even_l), (odd_h, odd_l), all_ref)
    place = place_ref[0]

    @pl.when(pl.program_id(0) == pl.num_programs(0) - 1)
    def _():
        n = all_ref.shape[1] // 2
        first_even = (place & 1) == 0

        def interleave(even, odd):
            a = jnp.where(first_even, even, odd)
            b = jnp.where(first_even, odd, even)
            return jnp.concatenate([a[:n], b[:n], a[n:], b[n:]], axis=0)

        low = place < FAST_WIDE // 2
        cross = interleave(cross_even[...], all_ref[:RANK].T)
        mixed = all_ref[RANK : RANK + 2 * n]
        other = interleave(
            jnp.concatenate([gram_even[...], mixed], axis=1),
            jnp.concatenate([mixed.T, all_ref[RANK + 2 * n :]], axis=1),
        ).T
        other = interleave(other[: 2 * n], other[2 * n :])
        corner = jnp.where(low, own_gram[...], other)
        corner_ref[...] = jnp.concatenate(
            [corner[:LANES, :LANES], corner[:LANES, LANES:], corner[LANES:, LANES:]], axis=0
        )
        below_ref[...] = jnp.where(low, cross, cross.T)


def whole(shape):
    return pl.BlockSpec(shape, lambda i: (0,) * len(shape))


def parts_of(x, size, first=0):
    return pl.BlockSpec((size,) + x.shape[1:], lambda i: (i + first,) + (0,) * (len(x.shape) - 1))


def call(
    kernel, name, steps, place, kept, blocks, split_blocks, kept_out, out, first=0, filled=(), scratch=(), flops=0
):
    pairs = blocks[0].shape[0] // 2 // steps
    moved = sum(4 * x.size for x in blocks) + sum(2 * s.size for s in out)
    return pl.pallas_call(
        kernel,
        grid=(steps,),
        in_specs=[pl.BlockSpec(memory_space=pltpu.SMEM)]
        + [whole(x.shape) for x in kept]
        + [parts_of(x, 2 * pairs) for x in blocks]
        + [parts_of(x, pairs, first) for x in split_blocks]
        + [pl.BlockSpec(memory_space=pl.ANY) for _ in filled],
        out_specs=[whole(s.shape) for s in kept_out] + [parts_of(s, pairs, first) for s in out],
        out_shape=list(kept_out) + list(out),
        scratch_shapes=list(scratch),
        input_output_aliases={
            1 + len(kept) + len(blocks) + len(split_blocks) + i: len(kept_out) + i for i in range(len(filled))
        },
        compiler_params=pltpu.CompilerParams(vmem_limit_bytes=VMEM_LIMIT),
        cost_estimate=pl.CostEstimate(flops=flops, bytes_accessed=moved, transcendentals=0),
        name=name,
    )(place, *kept, *blocks, *split_blocks, *filled)


def f32(*shape):
    return jax.ShapeDtypeStruct(shape, jnp.float32)


def halves(cells, rows, fields):
    return [jax.ShapeDtypeStruct((cells // 2, rows, 2 * fields), jnp.bfloat16)] * 2


def gram_of_own(place, blocks, steps):
    cells, rows, fields = blocks[0].shape
    n = rows * len(blocks)
    return call(
        own_kernel, "own_gram", steps, place, [], blocks, [], [f32(n, n)], halves(cells, n, fields),
        flops=8 * n * n * cells * fields,
    )


def gram_of_even(place, near, far, own, steps):
    cells, rows, fields = near.shape
    n = 2 * rows
    return call(
        even_kernel, "even_gram", steps, place, [], [near, far], own,
        [f32(n, 2 * n), f32(n, n)], halves(cells, n, fields), flops=24 * n * n * cells * fields,
    )


def gram_of_odd(place, near, far, own, even, steps):
    cells, rows, fields = near.shape
    n = 2 * rows
    return call(
        odd_kernel, "odd_gram", steps, place, [], [near, far], [*own, *even],
        [f32(4 * n, n)], halves(2 * own[0].shape[0], n, fields), flops=32 * n * n * cells * fields,
    )


def gram_of_last(place, kept, near, far, own, even, odd, steps):
    cells, rows, fields = near.shape
    n = 2 * rows
    pairs = cells // 2 // steps
    return call(
        last_kernel, "last_gram", steps, place, kept, [near, far], [*own, *even],
        [f32(3 * LANES, LANES), f32(RANK, RANK)], halves(2 * own[0].shape[0], n, fields), own[0].shape[0] // pairs - steps, odd,
        [pltpu.VMEM((4 * n, n), jnp.float32)], flops=32 * n * n * cells * fields,
    )


def over(step):
    axis, n, distance = step
    return functools.partial(lax.ppermute, axis_name=axis, perm=[(i, i ^ distance) for i in range(n)])


def sum_over_all(x, halved, doubled):
    sides = [(lax.axis_index(axis) & distance) != 0 for axis, _, distance in halved]
    for step, side in zip(halved, sides):
        n = x.shape[0] // 2
        keep = jnp.where(side, x[n:], x[:n])
        send = jnp.where(side, x[:n], x[n:])
        x = keep + over(step)(send)
    for step in doubled:
        x = x + over(step)(x)
    for step, side in reversed(list(zip(halved, sides))):
        got = over(step)(x)
        x = jnp.where(side, jnp.concatenate([got, x]), jnp.concatenate([x, got]))
    return x


def sum_both(corner, below, wide, narrow):
    core, y = ("narrow", narrow, 1), ("narrow", narrow, 2)
    x, z_near, z_far = [("wide", wide, 1 << b) for b in range(3)]
    corner = sum_over_all(corner, [core, y], [z_near, x, z_far])
    below = sum_over_all(below, [core, x], [y, z_far, z_near])
    return corner, below


PANEL = 64
SUB = 8


def refine_rsqrt(d):
    r = lax.rsqrt(d)
    return r * (1.5 - 0.5 * d * r * r)


def from_row(v, i):
    return jnp.broadcast_to(v[i : i + 1, :], (SUB, LANES))


def from_lane(v, c):
    return jnp.broadcast_to(v[:, c : c + 1], (SUB, LANES))


def full_product(a, b):
    def terms(x):
        high, rest = split_off(x)
        middle, rest = split_off(rest)
        return high, middle, rest.astype(jnp.bfloat16)

    (ah, am, al), (bh, bm, bl) = terms(a), terms(b)
    left = jnp.concatenate([ah, ah, am, ah, am, al], axis=0)
    right = jnp.concatenate([bh, bm, bh, bl, bm, bh], axis=0)
    return lax.dot_general(left, right, (((0,), (0,)), ((), ())), preferred_element_type=jnp.float32)


def cholesky_kernel(gram_ref, upper_ref, inverse_ref, work):
    n = upper_ref.shape[0]
    tiles = n // LANES
    groups = PANEL // SUB
    sub = lax.broadcasted_iota(jnp.int32, (SUB, LANES), 0)
    lane = lax.broadcasted_iota(jnp.int32, (SUB, LANES), 1)
    row_id = lax.broadcasted_iota(jnp.int32, (n, n), 0)
    col_id = lax.broadcasted_iota(jnp.int32, (n, n), 1)
    work[:LANES, :LANES] = gram_ref[:LANES]
    work[:LANES, LANES:n] = gram_ref[LANES : 2 * LANES]
    work[LANES:, LANES:n] = gram_ref[2 * LANES :]
    work[:, n:] = jnp.where(row_id == col_id, 1.0, 0.0)
    for top in range(0, n, PANEL):
        t0 = top // LANES
        cols = list(range(t0, tiles)) + [tiles + t for t in range(t0 + 1)]
        rows_of = lambda g: slice(top + SUB * g, top + SUB * (g + 1))
        lanes_of = lambda t: slice(LANES * t, LANES * (t + 1))
        grp = [[work[rows_of(g), lanes_of(t)] for t in cols] for g in range(groups)]
        pivots = [jnp.ones((SUB, LANES), jnp.float32) for _ in range(groups)]
        for g0 in range(groups):
            c0 = (top + SUB * g0) % LANES
            heads = [[from_lane(grp[g][0], c0 + j) for j in range(SUB)] for g in range(g0, groups)]
            for i in range(SUB):
                pivot = from_row(heads[0][i], i)
                pivots[g0] = jnp.where(sub == i, pivot, pivots[g0])
                inverse = pl.reciprocal(pivot, approx=True)
                head_row = {j: from_row(heads[0][j], i) for j in range(i + 1, SUB)}
                row = [from_row(v, i) for v in grp[g0]]
                for g in range(g0, groups):
                    head = heads[g - g0]
                    factor = head[i] * inverse
                    if g == g0:
                        factor = jnp.where(sub > i, factor, 0.0)
                    for j in range(i + 1, SUB):
                        head[j] = head[j] - factor * head_row[j]
                    grp[g] = [v - factor * r for v, r in zip(grp[g], row)]
        for g in range(groups):
            scale = refine_rsqrt(pivots[g])
            for v, t in zip(grp[g], cols):
                v = v * scale
                if t < tiles:
                    v = jnp.where(lane + LANES * t >= sub + (top + SUB * g), v, 0.0)
                work[rows_of(g), lanes_of(t)] = v
        for t in range(t0):
            work[top : top + PANEL, lanes_of(t)] = jnp.zeros((PANEL, LANES), jnp.float32)
        below = top + PANEL
        if below < n:
            lo, hi = LANES * t0, n + LANES * (t0 + 1)
            first = below // LANES * LANES
            update = full_product(work[top:below, first:n], work[top:below, lo:hi])
            work[below:, lo:hi] = work[below:, lo:hi] - update[below - first :, :]
    upper_ref[...] = work[:, :n]
    inverse_ref[...] = work[:, n:]


def cholesky(packed):
    n = RANK
    return pl.pallas_call(
        cholesky_kernel,
        out_shape=[f32(n, n)] * 2,
        scratch_shapes=[pltpu.VMEM((n, 2 * n), jnp.float32)],
        compiler_params=pltpu.CompilerParams(vmem_limit_bytes=VMEM_LIMIT),
        cost_estimate=pl.CostEstimate(flops=64 * n * n * n, bytes_accessed=12 * n * n, transcendentals=n),
        name="cholesky256",
    )(packed)


def core_kernel(place_ref, below, upper, inverse, own_h, own_l, even_h, even_l, odd_h, odd_l, *rest):
    factor_ref, out_ref, weights = rest

    @pl.when(pl.program_id(0) == 0)
    def _():
        left = upper[...]
        right = rows_dot(inverse[...], below[...], HIGHEST)
        squares = jnp.sum(left * left, axis=1, keepdims=True) + jnp.sum(right * right, axis=1, keepdims=True)
        length = jnp.sqrt(squares)
        left, right = left / length, right / length
        factor_ref[...] = jnp.concatenate([left, right], axis=1).T
        low = place_ref[0] < 4
        own = jnp.where(low, left, right)
        other = jnp.where(low, right, left)
        n = RANK // 4
        first = jnp.concatenate([other[:, :n], other[:, 2 * n : 3 * n]], axis=1)
        second = jnp.concatenate([other[:, n : 2 * n], other[:, 3 * n :]], axis=1)
        first_even = (place_ref[0] & 1) == 0
        even = jnp.where(first_even, first, second)
        odd = jnp.where(first_even, second, first)
        high, small = split(jnp.concatenate([own, even, odd], axis=1))
        weights[...] = jnp.concatenate([high, small, high], axis=1)

    w = weights[...]
    for t in range(own_h.shape[0]):
        high = [r[t] for r in (own_h, even_h, odd_h)]
        small = [r[t] for r in (own_l, even_l, odd_l)]
        both = jnp.dot(w, jnp.concatenate(high + high + small, axis=0), preferred_element_type=jnp.float32)
        out_ref[:, 0, 2 * t, :] = both[:, :LANES]
        out_ref[:, 0, 2 * t + 1, :] = both[:, LANES:]


def core_and_factor(place, kept, streamed, ny, nz, fields):
    size = sum(x.shape[1] for x in streamed) // 2
    return pl.pallas_call(
        core_kernel,
        grid=(ny,),
        in_specs=[pl.BlockSpec(memory_space=pltpu.SMEM)]
        + [whole(x.shape) for x in kept]
        + [parts_of(x, nz // 2) for x in streamed],
        out_specs=[whole((size, RANK)), pl.BlockSpec((RANK, 1, nz, fields), lambda i: (0, i, 0, 0))],
        out_shape=[f32(size, RANK), f32(RANK, ny, nz, fields)],
        scratch_shapes=[pltpu.VMEM((RANK, 3 * size), jnp.bfloat16)],
        compiler_params=pltpu.CompilerParams(vmem_limit_bytes=VMEM_LIMIT),
        cost_estimate=pl.CostEstimate(
            flops=6 * size * RANK * ny * nz * fields,
            bytes_accessed=4 * (size + RANK) * ny * nz * fields,
            transcendentals=0,
        ),
        name="core",
    )(place, *kept, *streamed)


def tie(x, *deps):
    return lax.optimization_barrier((x,) + deps)[0]


def block_for(snapshot, device, nz):
    rows, ny, _, fields = snapshot.shape
    cut = lax.dynamic_slice_in_dim(snapshot, device * nz, nz, axis=2)
    return cut.transpose(1, 2, 0, 3).reshape(ny * nz, rows, fields)


def on_device_blocks(snapshot, wide, narrow):
    ny, nz = snapshot.shape[1], snapshot.shape[2] // wide
    here = lax.axis_index("wide")
    place = here.astype(jnp.int32).reshape(1)
    first = block_for(snapshot, here ^ 6, nz)
    snapshot = tie(snapshot, first)
    got = {}
    send = lambda k, *deps: over(("wide", wide, k))(tie(block_for(snapshot, here ^ k, nz), *deps))
    got[6] = over(("wide", wide, 6))(first)
    got[4], got[2], got[1] = send(4), send(2), send(1)
    got[3] = send(3, got[6])
    split_at = (ny - LATE) * nz
    blocks, late = {}, {}
    for k, after in ((5, 6), (7, 4)):
        block = tie(block_for(snapshot, here ^ k, nz), got[after])
        got[k] = over(("wide", wide, k))(block[:split_at])
        blocks[k] = block[split_at:]
    late[5] = over(("wide", wide, 5))(tie(blocks[5], got[7]))
    late[7] = over(("wide", wide, 7))(tie(blocks[7], got[7]))
    got[0] = block_for(snapshot, here, nz)
    own_gram, *own = gram_of_own(place, [got[k] for k in range(4)], ny)
    cross_even, gram_even, *even = gram_of_even(place, got[4], got[6], own, ny)
    all_odd, *odd = gram_of_odd(place, got[5], got[7], own, even, ny - LATE)
    kept = [own_gram, cross_even, gram_even, all_odd]
    corner, below, *odd = gram_of_last(place, kept, late[5], late[7], own, even, odd, LATE * LATE_STEPS)
    corner, below = sum_both(corner, below, wide, narrow)
    upper, inverse = cholesky(corner)
    factor, core = core_and_factor(
        place, [below, upper, inverse], [*own, *even, *odd], ny, nz, snapshot.shape[3]
    )
    return core, factor


def on_device_any(snapshot):
    regrouped = lax.all_to_all(snapshot, "wide", split_axis=2, concat_axis=0, tiled=True)
    rows_all = regrouped.shape[0]
    unfold = regrouped.reshape(rows_all, -1)
    gram = lax.dot_general(
        unfold, unfold[:RANK], (((1,), (1,)), ((), ())), precision=HIGHEST, preferred_element_type=jnp.float32
    )
    gram = lax.psum(lax.psum(gram, "narrow"), "wide")
    lower = jnp.linalg.cholesky(gram[:RANK])
    upper = jnp.concatenate(
        [lower.T, lax.linalg.triangular_solve(lower, gram[RANK:].T, left_side=True, lower=True)], axis=1
    )
    lengths = jnp.sqrt(jnp.sum(upper * upper, axis=1))
    factor = (upper / lengths[:, None]).T
    core = jnp.dot(factor.T, unfold, precision=HIGHEST, preferred_element_type=jnp.float32)
    return core.reshape((RANK,) + regrouped.shape[1:]), factor


def solution(mesh):
    wide, narrow = mesh.shape["wide"], mesh.shape["narrow"]
    if (wide, narrow) == (FAST_WIDE, FAST_NARROW):
        on_device = functools.partial(on_device_blocks, wide=wide, narrow=narrow)
    else:
        on_device = on_device_any
    return jax.shard_map(
        on_device,
        mesh=mesh,
        in_specs=(P("wide", "narrow", None, None),),
        out_specs=(P(None, "narrow", "wide", None), P()),
        check_vma=False,
    )
```

```python
import functools

import jax
import jax.numpy as jnp
from jax import lax
from jax.experimental import pallas as pl
from jax.experimental.pallas import tpu as pltpu
from jax.sharding import PartitionSpec as P

RANK = 256
LANES = 128
FAST_WIDE, FAST_NARROW = 8, 4
LATE = 1
LATE_STEPS = 2
HIGHEST = lax.Precision.HIGHEST
VMEM_LIMIT = 16 * 1024 * 1024


def split_off(x):
    high = x.astype(jnp.bfloat16)
    return high, x - high.astype(jnp.float32)


def split(x):
    high, rest = split_off(x)
    return high, rest.astype(jnp.bfloat16)


def by_device(place, blocks):
    distance = 1
    while distance < len(blocks):
        flag = (place & distance) != 0
        blocks = [jnp.where(flag, blocks[i ^ distance], blocks[i]) for i in range(len(blocks))]
        distance *= 2
    return blocks


def two_cells(place, refs, t):
    sides = [jnp.concatenate(by_device(place, [r[c] for r in refs]), axis=0) for c in (2 * t, 2 * t + 1)]
    return jnp.concatenate(sides, axis=1)


def rows_dot(a, b, precision=None):
    return lax.dot_general(
        a, b, (((1,), (1,)), ((), ())), precision=precision, preferred_element_type=jnp.float32
    )


def product(a, b):
    (ah, al), (bh, bl) = a, b
    left = jnp.concatenate([ah, ah, al, al], axis=1)
    right = jnp.concatenate([bh, bl, bh, bl], axis=1)
    return rows_dot(left, right)


def read(pair, t):
    return pair[0][t], pair[1][t]


def write(pair, t, value):
    pair[0][t], pair[1][t] = value


def add_to(ref, value):
    ref[...] = ref[...] + value


def start_at_zero(*refs):
    @pl.when(pl.program_id(0) == 0)
    def _():
        for ref in refs:
            ref[...] = jnp.zeros_like(ref)


def own_kernel(place_ref, *refs):
    blocks, (gram_ref, *own) = refs[:-3], refs[-3:]
    start_at_zero(gram_ref)
    for t in range(blocks[0].shape[0] // 2):
        x = split(two_cells(place_ref[0], blocks, t))
        write(own, t, x)
        add_to(gram_ref, product(x, x))


def even_kernel(place_ref, near, far, own_h, own_l, cross_ref, gram_ref, *even):
    start_at_zero(cross_ref, gram_ref)
    place = place_ref[0] // 2
    for t in range(near.shape[0] // 2):
        x = split(two_cells(place, (near, far), t))
        write(even, t, x)
        add_to(cross_ref, product(x, read((own_h, own_l), t)))
        add_to(gram_ref, product(x, x))


def add_odd(place_ref, near, far, own, even, odd, all_ref):
    for t in range(near.shape[0] // 2):
        x = split(two_cells(place_ref[0] // 2, (near, far), t))
        write(odd, t, x)
        both = jnp.concatenate(x, axis=0)
        n = both.shape[0] // 2
        high = rows_dot(jnp.concatenate([own[0][t], even[0][t], x[0]], axis=0), both)
        low = rows_dot(jnp.concatenate([own[1][t], even[1][t], x[1]], axis=0), both)
        add_to(all_ref, (high[:, :n] + high[:, n:]) + (low[:, :n] + low[:, n:]))


def odd_kernel(place_ref, near, far, own_h, own_l, even_h, even_l, all_ref, odd_h, odd_l):
    start_at_zero(all_ref)
    add_odd(place_ref, near, far, (own_h, own_l), (even_h, even_l), (odd_h, odd_l), all_ref)


def last_kernel(
    place_ref, own_gram, cross_even, gram_even, all_odd, near, far, own_h, own_l, even_h, even_l, _, __,
    corner_ref, below_ref, odd_h, odd_l, all_ref,
):
    @pl.when(pl.program_id(0) == 0)
    def _():
        all_ref[...] = all_odd[...]

    add_odd(place_ref, near, far, (own_h, own_l), (even_h, even_l), (odd_h, odd_l), all_ref)
    place = place_ref[0]

    @pl.when(pl.program_id(0) == pl.num_programs(0) - 1)
    def _():
        n = all_ref.shape[1] // 2
        first_even = (place & 1) == 0

        def interleave(even, odd):
            a = jnp.where(first_even, even, odd)
            b = jnp.where(first_even, odd, even)
            return jnp.concatenate([a[:n], b[:n], a[n:], b[n:]], axis=0)

        low = place < FAST_WIDE // 2
        cross = interleave(cross_even[...], all_ref[:RANK].T)
        mixed = all_ref[RANK : RANK + 2 * n]
        other = interleave(
            jnp.concatenate([gram_even[...], mixed], axis=1),
            jnp.concatenate([mixed.T, all_ref[RANK + 2 * n :]], axis=1),
        ).T
        other = interleave(other[: 2 * n], other[2 * n :])
        corner = jnp.where(low, own_gram[...], other)
        corner_ref[...] = jnp.concatenate(
            [corner[:LANES, :LANES], corner[:LANES, LANES:], corner[LANES:, LANES:]], axis=0
        )
        below_ref[...] = jnp.where(low, cross, cross.T)


def whole(shape):
    return pl.BlockSpec(shape, lambda i: (0,) * len(shape))


def parts_of(x, size, first=0):
    return pl.BlockSpec((size,) + x.shape[1:], lambda i: (i + first,) + (0,) * (len(x.shape) - 1))


def call(
    kernel, name, steps, place, kept, blocks, split_blocks, kept_out, out, first=0, filled=(), scratch=(), flops=0
):
    pairs = blocks[0].shape[0] // 2 // steps
    moved = sum(4 * x.size for x in blocks) + sum(2 * s.size for s in out)
    return pl.pallas_call(
        kernel,
        grid=(steps,),
        in_specs=[pl.BlockSpec(memory_space=pltpu.SMEM)]
        + [whole(x.shape) for x in kept]
        + [parts_of(x, 2 * pairs) for x in blocks]
        + [parts_of(x, pairs, first) for x in split_blocks]
        + [pl.BlockSpec(memory_space=pl.ANY) for _ in filled],
        out_specs=[whole(s.shape) for s in kept_out] + [parts_of(s, pairs, first) for s in out],
        out_shape=list(kept_out) + list(out),
        scratch_shapes=list(scratch),
        input_output_aliases={
            1 + len(kept) + len(blocks) + len(split_blocks) + i: len(kept_out) + i for i in range(len(filled))
        },
        compiler_params=pltpu.CompilerParams(vmem_limit_bytes=VMEM_LIMIT),
        cost_estimate=pl.CostEstimate(flops=flops, bytes_accessed=moved, transcendentals=0),
        name=name,
    )(place, *kept, *blocks, *split_blocks, *filled)


def f32(*shape):
    return jax.ShapeDtypeStruct(shape, jnp.float32)


def halves(cells, rows, fields):
    return [jax.ShapeDtypeStruct((cells // 2, rows, 2 * fields), jnp.bfloat16)] * 2


def gram_of_own(place, blocks, steps):
    cells, rows, fields = blocks[0].shape
    n = rows * len(blocks)
    return call(
        own_kernel, "own_gram", steps, place, [], blocks, [], [f32(n, n)], halves(cells, n, fields),
        flops=8 * n * n * cells * fields,
    )


def gram_of_even(place, near, far, own, steps):
    cells, rows, fields = near.shape
    n = 2 * rows
    return call(
        even_kernel, "even_gram", steps, place, [], [near, far], own,
        [f32(n, 2 * n), f32(n, n)], halves(cells, n, fields), flops=24 * n * n * cells * fields,
    )


def gram_of_odd(place, near, far, own, even, steps):
    cells, rows, fields = near.shape
    n = 2 * rows
    return call(
        odd_kernel, "odd_gram", steps, place, [], [near, far], [*own, *even],
        [f32(4 * n, n)], halves(2 * own[0].shape[0], n, fields), flops=32 * n * n * cells * fields,
    )


def gram_of_last(place, kept, near, far, own, even, odd, steps):
    cells, rows, fields = near.shape
    n = 2 * rows
    pairs = cells // 2 // steps
    return call(
        last_kernel, "last_gram", steps, place, kept, [near, far], [*own, *even],
        [f32(3 * LANES, LANES), f32(RANK, RANK)], halves(2 * own[0].shape[0], n, fields), own[0].shape[0] // pairs - steps, odd,
        [pltpu.VMEM((4 * n, n), jnp.float32)], flops=32 * n * n * cells * fields,
    )


def over(step):
    axis, n, distance = step
    return functools.partial(lax.ppermute, axis_name=axis, perm=[(i, i ^ distance) for i in range(n)])


def sum_over_all(x, halved, doubled):
    sides = [(lax.axis_index(axis) & distance) != 0 for axis, _, distance in halved]
    for step, side in zip(halved, sides):
        n = x.shape[0] // 2
        keep = jnp.where(side, x[n:], x[:n])
        send = jnp.where(side, x[:n], x[n:])
        x = keep + over(step)(send)
    for step in doubled:
        x = x + over(step)(x)
    for step, side in reversed(list(zip(halved, sides))):
        got = over(step)(x)
        x = jnp.where(side, jnp.concatenate([got, x]), jnp.concatenate([x, got]))
    return x


def sum_both(corner, below, wide, narrow):
    core, y = ("narrow", narrow, 1), ("narrow", narrow, 2)
    x, z_near, z_far = [("wide", wide, 1 << b) for b in range(3)]
    corner = sum_over_all(corner, [core, y], [z_near, x, z_far])
    below = sum_over_all(below, [core, x], [y, z_far, z_near])
    return corner, below


PANEL = 64
SUB = 8


def refine_rsqrt(d):
    r = lax.rsqrt(d)
    return r * (1.5 - 0.5 * d * r * r)


def from_row(v, i):
    return jnp.broadcast_to(v[i : i + 1, :], (SUB, LANES))


def from_lane(v, c):
    return jnp.broadcast_to(v[:, c : c + 1], (SUB, LANES))


def full_product(a, b):
    def terms(x):
        high, rest = split_off(x)
        middle, rest = split_off(rest)
        return high, middle, rest.astype(jnp.bfloat16)

    (ah, am, al), (bh, bm, bl) = terms(a), terms(b)
    left = jnp.concatenate([ah, ah, am, ah, am, al], axis=0)
    right = jnp.concatenate([bh, bm, bh, bl, bm, bh], axis=0)
    return lax.dot_general(left, right, (((0,), (0,)), ((), ())), preferred_element_type=jnp.float32)


def cholesky_kernel(gram_ref, upper_ref, inverse_ref, work):
    n = upper_ref.shape[0]
    tiles = n // LANES
    groups = PANEL // SUB
    sub = lax.broadcasted_iota(jnp.int32, (SUB, LANES), 0)
    lane = lax.broadcasted_iota(jnp.int32, (SUB, LANES), 1)
    row_id = lax.broadcasted_iota(jnp.int32, (n, n), 0)
    col_id = lax.broadcasted_iota(jnp.int32, (n, n), 1)
    work[:LANES, :LANES] = gram_ref[:LANES]
    work[:LANES, LANES:n] = gram_ref[LANES : 2 * LANES]
    work[LANES:, LANES:n] = gram_ref[2 * LANES :]
    work[:, n:] = jnp.where(row_id == col_id, 1.0, 0.0)
    for top in range(0, n, PANEL):
        t0 = top // LANES
        cols = list(range(t0, tiles)) + [tiles + t for t in range(t0 + 1)]
        rows_of = lambda g: slice(top + SUB * g, top + SUB * (g + 1))
        lanes_of = lambda t: slice(LANES * t, LANES * (t + 1))
        grp = [[work[rows_of(g), lanes_of(t)] for t in cols] for g in range(groups)]
        pivots = [jnp.ones((SUB, LANES), jnp.float32) for _ in range(groups)]
        for g0 in range(groups):
            c0 = (top + SUB * g0) % LANES
            heads = [[from_lane(grp[g][0], c0 + j) for j in range(SUB)] for g in range(g0, groups)]
            for i in range(SUB):
                pivot = from_row(heads[0][i], i)
                pivots[g0] = jnp.where(sub == i, pivot, pivots[g0])
                inverse = pl.reciprocal(pivot, approx=True)
                head_row = {j: from_row(heads[0][j], i) for j in range(i + 1, SUB)}
                row = [from_row(v, i) for v in grp[g0]]
                for g in range(g0, groups):
                    head = heads[g - g0]
                    factor = head[i] * inverse
                    if g == g0:
                        factor = jnp.where(sub > i, factor, 0.0)
                    for j in range(i + 1, SUB):
                        head[j] = head[j] - factor * head_row[j]
                    grp[g] = [v - factor * r for v, r in zip(grp[g], row)]
        for g in range(groups):
            scale = refine_rsqrt(pivots[g])
            for v, t in zip(grp[g], cols):
                v = v * scale
                if t < tiles:
                    v = jnp.where(lane + LANES * t >= sub + (top + SUB * g), v, 0.0)
                work[rows_of(g), lanes_of(t)] = v
        for t in range(t0):
            work[top : top + PANEL, lanes_of(t)] = jnp.zeros((PANEL, LANES), jnp.float32)
        below = top + PANEL
        if below < n:
            lo, hi = LANES * t0, n + LANES * (t0 + 1)
            first = below // LANES * LANES
            update = full_product(work[top:below, first:n], work[top:below, lo:hi])
            work[below:, lo:hi] = work[below:, lo:hi] - update[below - first :, :]
    upper_ref[...] = work[:, :n]
    inverse_ref[...] = work[:, n:]


def cholesky(packed):
    n = RANK
    return pl.pallas_call(
        cholesky_kernel,
        out_shape=[f32(n, n)] * 2,
        scratch_shapes=[pltpu.VMEM((n, 2 * n), jnp.float32)],
        compiler_params=pltpu.CompilerParams(vmem_limit_bytes=VMEM_LIMIT),
        cost_estimate=pl.CostEstimate(flops=64 * n * n * n, bytes_accessed=12 * n * n, transcendentals=n),
        name="cholesky256",
    )(packed)


def core_kernel(place_ref, below, upper, inverse, own_h, own_l, even_h, even_l, odd_h, odd_l, *rest):
    factor_ref, out_ref, weights = rest

    @pl.when(pl.program_id(0) == 0)
    def _():
        left = upper[...]
        right = rows_dot(inverse[...], below[...], HIGHEST)
        squares = jnp.sum(left * left, axis=1, keepdims=True) + jnp.sum(right * right, axis=1, keepdims=True)
        length = jnp.sqrt(squares)
        left, right = left / length, right / length
        factor_ref[...] = jnp.concatenate([left, right], axis=1).T
        low = place_ref[0] < 4
        own = jnp.where(low, left, right)
        other = jnp.where(low, right, left)
        n = RANK // 4
        first = jnp.concatenate([other[:, :n], other[:, 2 * n : 3 * n]], axis=1)
        second = jnp.concatenate([other[:, n : 2 * n], other[:, 3 * n :]], axis=1)
        first_even = (place_ref[0] & 1) == 0
        even = jnp.where(first_even, first, second)
        odd = jnp.where(first_even, second, first)
        high, small = split(jnp.concatenate([own, even, odd], axis=1))
        weights[...] = jnp.concatenate([high, small, high], axis=1)

    w = weights[...]
    cells = []
    for t in range(own_h.shape[0]):
        high = [r[t] for r in (own_h, even_h, odd_h)]
        small = [r[t] for r in (own_l, even_l, odd_l)]
        both = jnp.dot(w, jnp.concatenate(high + high + small, axis=0), preferred_element_type=jnp.float32)
        cells += [both[:, :LANES], both[:, LANES:]]
    out_ref[:, 0, :, :] = jnp.swapaxes(jnp.stack(cells, axis=0), 0, 1)


def core_and_factor(place, kept, streamed, ny, nz, fields):
    size = sum(x.shape[1] for x in streamed) // 2
    return pl.pallas_call(
        core_kernel,
        grid=(ny,),
        in_specs=[pl.BlockSpec(memory_space=pltpu.SMEM)]
        + [whole(x.shape) for x in kept]
        + [parts_of(x, nz // 2) for x in streamed],
        out_specs=[whole((size, RANK)), pl.BlockSpec((RANK, 1, nz, fields), lambda i: (0, i, 0, 0))],
        out_shape=[f32(size, RANK), f32(RANK, ny, nz, fields)],
        scratch_shapes=[pltpu.VMEM((RANK, 3 * size), jnp.bfloat16)],
        compiler_params=pltpu.CompilerParams(vmem_limit_bytes=VMEM_LIMIT),
        cost_estimate=pl.CostEstimate(
            flops=6 * size * RANK * ny * nz * fields,
            bytes_accessed=4 * (size + RANK) * ny * nz * fields,
            transcendentals=0,
        ),
        name="core",
    )(place, *kept, *streamed)


def tie(x, *deps):
    return lax.optimization_barrier((x,) + deps)[0]


def block_for(snapshot, device, nz):
    rows, ny, _, fields = snapshot.shape
    cut = lax.dynamic_slice_in_dim(snapshot, device * nz, nz, axis=2)
    return cut.transpose(1, 2, 0, 3).reshape(ny * nz, rows, fields)


def on_device_blocks(snapshot, wide, narrow):
    ny, nz = snapshot.shape[1], snapshot.shape[2] // wide
    here = lax.axis_index("wide")
    place = here.astype(jnp.int32).reshape(1)
    first = block_for(snapshot, here ^ 6, nz)
    snapshot = tie(snapshot, first)
    got = {}
    send = lambda k, *deps: over(("wide", wide, k))(tie(block_for(snapshot, here ^ k, nz), *deps))
    got[6] = over(("wide", wide, 6))(first)
    got[4], got[2], got[1] = send(4), send(2), send(1)
    got[3] = send(3, got[6])
    split_at = (ny - LATE) * nz
    blocks, late = {}, {}
    for k, after in ((5, 6), (7, 4)):
        block = tie(block_for(snapshot, here ^ k, nz), got[after])
        got[k] = over(("wide", wide, k))(block[:split_at])
        blocks[k] = block[split_at:]
    late[5] = over(("wide", wide, 5))(tie(blocks[5], got[7]))
    late[7] = over(("wide", wide, 7))(tie(blocks[7], got[7]))
    got[0] = block_for(snapshot, here, nz)
    own_gram, *own = gram_of_own(place, [got[k] for k in range(4)], ny)
    cross_even, gram_even, *even = gram_of_even(place, got[4], got[6], own, ny)
    all_odd, *odd = gram_of_odd(place, got[5], got[7], own, even, ny - LATE)
    kept = [own_gram, cross_even, gram_even, all_odd]
    corner, below, *odd = gram_of_last(place, kept, late[5], late[7], own, even, odd, LATE * LATE_STEPS)
    corner, below = sum_both(corner, below, wide, narrow)
    upper, inverse = cholesky(corner)
    factor, core = core_and_factor(
        place, [below, upper, inverse], [*own, *even, *odd], ny, nz, snapshot.shape[3]
    )
    return core, factor


def on_device_any(snapshot):
    regrouped = lax.all_to_all(snapshot, "wide", split_axis=2, concat_axis=0, tiled=True)
    rows_all = regrouped.shape[0]
    unfold = regrouped.reshape(rows_all, -1)
    gram = lax.dot_general(
        unfold, unfold[:RANK], (((1,), (1,)), ((), ())), precision=HIGHEST, preferred_element_type=jnp.float32
    )
    gram = lax.psum(lax.psum(gram, "narrow"), "wide")
    lower = jnp.linalg.cholesky(gram[:RANK])
    upper = jnp.concatenate(
        [lower.T, lax.linalg.triangular_solve(lower, gram[RANK:].T, left_side=True, lower=True)], axis=1
    )
    lengths = jnp.sqrt(jnp.sum(upper * upper, axis=1))
    factor = (upper / lengths[:, None]).T
    core = jnp.dot(factor.T, unfold, precision=HIGHEST, preferred_element_type=jnp.float32)
    return core.reshape((RANK,) + regrouped.shape[1:]), factor


def solution(mesh):
    wide, narrow = mesh.shape["wide"], mesh.shape["narrow"]
    if (wide, narrow) == (FAST_WIDE, FAST_NARROW):
        on_device = functools.partial(on_device_blocks, wide=wide, narrow=narrow)
    else:
        on_device = on_device_any
    return jax.shard_map(
        on_device,
        mesh=mesh,
        in_specs=(P("wide", "narrow", None, None),),
        out_specs=(P(None, "narrow", "wide", None), P()),
        check_vma=False,
    )
```

```python
import functools

import jax
import jax.numpy as jnp
from jax import lax
from jax.experimental import pallas as pl
from jax.experimental.pallas import tpu as pltpu
from jax.sharding import PartitionSpec as P

RANK = 256
LANES = 128
FAST_WIDE, FAST_NARROW = 8, 4
LATE = 1
LATE_STEPS = 1
HIGHEST = lax.Precision.HIGHEST
VMEM_LIMIT = 16 * 1024 * 1024


def split_off(x):
    high = x.astype(jnp.bfloat16)
    return high, x - high.astype(jnp.float32)


def split(x):
    high, rest = split_off(x)
    return high, rest.astype(jnp.bfloat16)


def by_device(place, blocks):
    distance = 1
    while distance < len(blocks):
        flag = (place & distance) != 0
        blocks = [jnp.where(flag, blocks[i ^ distance], blocks[i]) for i in range(len(blocks))]
        distance *= 2
    return blocks


def two_cells(place, refs, t):
    sides = [jnp.concatenate(by_device(place, [r[c] for r in refs]), axis=0) for c in (2 * t, 2 * t + 1)]
    return jnp.concatenate(sides, axis=1)


def rows_dot(a, b, precision=None):
    return lax.dot_general(
        a, b, (((1,), (1,)), ((), ())), precision=precision, preferred_element_type=jnp.float32
    )


def product(a, b):
    (ah, al), (bh, bl) = a, b
    left = jnp.concatenate([ah, ah, al, al], axis=1)
    right = jnp.concatenate([bh, bl, bh, bl], axis=1)
    return rows_dot(left, right)


def read(pair, t):
    return pair[0][t], pair[1][t]


def write(pair, t, value):
    pair[0][t], pair[1][t] = value


def add_to(ref, value):
    ref[...] = ref[...] + value


def start_at_zero(*refs):
    @pl.when(pl.program_id(0) == 0)
    def _():
        for ref in refs:
            ref[...] = jnp.zeros_like(ref)


def own_kernel(place_ref, *refs):
    blocks, (gram_ref, *own) = refs[:-3], refs[-3:]
    start_at_zero(gram_ref)
    for t in range(blocks[0].shape[0] // 2):
        x = split(two_cells(place_ref[0], blocks, t))
        write(own, t, x)
        add_to(gram_ref, product(x, x))


def even_kernel(place_ref, near, far, own_h, own_l, cross_ref, gram_ref, *even):
    start_at_zero(cross_ref, gram_ref)
    place = place_ref[0] // 2
    for t in range(near.shape[0] // 2):
        x = split(two_cells(place, (near, far), t))
        write(even, t, x)
        add_to(cross_ref, product(x, read((own_h, own_l), t)))
        add_to(gram_ref, product(x, x))


def add_odd(place_ref, near, far, own, even, odd, all_ref):
    for t in range(near.shape[0] // 2):
        x = split(two_cells(place_ref[0] // 2, (near, far), t))
        write(odd, t, x)
        both = jnp.concatenate(x, axis=0)
        n = both.shape[0] // 2
        high = rows_dot(jnp.concatenate([own[0][t], even[0][t], x[0]], axis=0), both)
        low = rows_dot(jnp.concatenate([own[1][t], even[1][t], x[1]], axis=0), both)
        add_to(all_ref, (high[:, :n] + high[:, n:]) + (low[:, :n] + low[:, n:]))


def odd_kernel(place_ref, near, far, own_h, own_l, even_h, even_l, all_ref, odd_h, odd_l):
    start_at_zero(all_ref)
    add_odd(place_ref, near, far, (own_h, own_l), (even_h, even_l), (odd_h, odd_l), all_ref)


def last_kernel(
    place_ref, own_gram, cross_even, gram_even, all_odd, near, far, own_h, own_l, even_h, even_l, _, __,
    corner_ref, below_ref, odd_h, odd_l, all_ref,
):
    @pl.when(pl.program_id(0) == 0)
    def _():
        all_ref[...] = all_odd[...]

    add_odd(place_ref, near, far, (own_h, own_l), (even_h, even_l), (odd_h, odd_l), all_ref)
    place = place_ref[0]

    @pl.when(pl.program_id(0) == pl.num_programs(0) - 1)
    def _():
        n = all_ref.shape[1] // 2
        first_even = (place & 1) == 0

        def interleave(even, odd):
            a = jnp.where(first_even, even, odd)
            b = jnp.where(first_even, odd, even)
            return jnp.concatenate([a[:n], b[:n], a[n:], b[n:]], axis=0)

        low = place < FAST_WIDE // 2
        cross = interleave(cross_even[...], all_ref[:RANK].T)
        mixed = all_ref[RANK : RANK + 2 * n]
        other = interleave(
            jnp.concatenate([gram_even[...], mixed], axis=1),
            jnp.concatenate([mixed.T, all_ref[RANK + 2 * n :]], axis=1),
        ).T
        other = interleave(other[: 2 * n], other[2 * n :])
        corner = jnp.where(low, own_gram[...], other)
        corner_ref[...] = jnp.concatenate(
            [corner[:LANES, :LANES], corner[:LANES, LANES:], corner[LANES:, LANES:]], axis=0
        )
        below_ref[...] = jnp.where(low, cross, cross.T)


def whole(shape):
    return pl.BlockSpec(shape, lambda i: (0,) * len(shape))


def parts_of(x, size, first=0):
    return pl.BlockSpec((size,) + x.shape[1:], lambda i: (i + first,) + (0,) * (len(x.shape) - 1))


def call(
    kernel, name, steps, place, kept, blocks, split_blocks, kept_out, out, first=0, filled=(), scratch=(), flops=0
):
    pairs = blocks[0].shape[0] // 2 // steps
    moved = sum(4 * x.size for x in blocks) + sum(2 * s.size for s in out)
    return pl.pallas_call(
        kernel,
        grid=(steps,),
        in_specs=[pl.BlockSpec(memory_space=pltpu.SMEM)]
        + [whole(x.shape) for x in kept]
        + [parts_of(x, 2 * pairs) for x in blocks]
        + [parts_of(x, pairs, first) for x in split_blocks]
        + [pl.BlockSpec(memory_space=pl.ANY) for _ in filled],
        out_specs=[whole(s.shape) for s in kept_out] + [parts_of(s, pairs, first) for s in out],
        out_shape=list(kept_out) + list(out),
        scratch_shapes=list(scratch),
        input_output_aliases={
            1 + len(kept) + len(blocks) + len(split_blocks) + i: len(kept_out) + i for i in range(len(filled))
        },
        compiler_params=pltpu.CompilerParams(vmem_limit_bytes=VMEM_LIMIT),
        cost_estimate=pl.CostEstimate(flops=flops, bytes_accessed=moved, transcendentals=0),
        name=name,
    )(place, *kept, *blocks, *split_blocks, *filled)


def f32(*shape):
    return jax.ShapeDtypeStruct(shape, jnp.float32)


def halves(cells, rows, fields):
    return [jax.ShapeDtypeStruct((cells // 2, rows, 2 * fields), jnp.bfloat16)] * 2


def gram_of_own(place, blocks, steps):
    cells, rows, fields = blocks[0].shape
    n = rows * len(blocks)
    return call(
        own_kernel, "own_gram", steps, place, [], blocks, [], [f32(n, n)], halves(cells, n, fields),
        flops=8 * n * n * cells * fields,
    )


def gram_of_even(place, near, far, own, steps):
    cells, rows, fields = near.shape
    n = 2 * rows
    return call(
        even_kernel, "even_gram", steps, place, [], [near, far], own,
        [f32(n, 2 * n), f32(n, n)], halves(cells, n, fields), flops=24 * n * n * cells * fields,
    )


def gram_of_odd(place, near, far, own, even, steps):
    cells, rows, fields = near.shape
    n = 2 * rows
    return call(
        odd_kernel, "odd_gram", steps, place, [], [near, far], [*own, *even],
        [f32(4 * n, n)], halves(2 * own[0].shape[0], n, fields), flops=32 * n * n * cells * fields,
    )


def gram_of_last(place, kept, near, far, own, even, odd, steps):
    cells, rows, fields = near.shape
    n = 2 * rows
    pairs = cells // 2 // steps
    return call(
        last_kernel, "last_gram", steps, place, kept, [near, far], [*own, *even],
        [f32(3 * LANES, LANES), f32(RANK, RANK)], halves(2 * own[0].shape[0], n, fields), own[0].shape[0] // pairs - steps, odd,
        [pltpu.VMEM((4 * n, n), jnp.float32)], flops=32 * n * n * cells * fields,
    )


def over(step):
    axis, n, distance = step
    return functools.partial(lax.ppermute, axis_name=axis, perm=[(i, i ^ distance) for i in range(n)])


def sum_over_all(x, halved, doubled):
    sides = [(lax.axis_index(axis) & distance) != 0 for axis, _, distance in halved]
    for step, side in zip(halved, sides):
        n = x.shape[0] // 2
        keep = jnp.where(side, x[n:], x[:n])
        send = jnp.where(side, x[:n], x[n:])
        x = keep + over(step)(send)
    for step in doubled:
        x = x + over(step)(x)
    for step, side in reversed(list(zip(halved, sides))):
        got = over(step)(x)
        x = jnp.where(side, jnp.concatenate([got, x]), jnp.concatenate([x, got]))
    return x


def sum_both(corner, below, wide, narrow):
    core, y = ("narrow", narrow, 1), ("narrow", narrow, 2)
    x, z_near, z_far = [("wide", wide, 1 << b) for b in range(3)]
    corner = sum_over_all(corner, [core, y], [z_near, x, z_far])
    below = sum_over_all(below, [core, x], [y, z_far, z_near])
    return corner, below


PANEL = 64
SUB = 8


def refine_rsqrt(d):
    r = lax.rsqrt(d)
    return r * (1.5 - 0.5 * d * r * r)


def from_row(v, i):
    return jnp.broadcast_to(v[i : i + 1, :], (SUB, LANES))


def from_lane(v, c):
    return jnp.broadcast_to(v[:, c : c + 1], (SUB, LANES))


def full_product(a, b):
    def terms(x):
        high, rest = split_off(x)
        middle, rest = split_off(rest)
        return high, middle, rest.astype(jnp.bfloat16)

    (ah, am, al), (bh, bm, bl) = terms(a), terms(b)
    left = jnp.concatenate([ah, ah, am, ah, am, al], axis=0)
    right = jnp.concatenate([bh, bm, bh, bl, bm, bh], axis=0)
    return lax.dot_general(left, right, (((0,), (0,)), ((), ())), preferred_element_type=jnp.float32)


def cholesky_kernel(gram_ref, upper_ref, inverse_ref):
    n = upper_ref.shape[0]
    tiles = n // LANES
    groups = PANEL // SUB
    sub = lax.broadcasted_iota(jnp.int32, (SUB, LANES), 0)
    lane = lax.broadcasted_iota(jnp.int32, (SUB, LANES), 1)
    row_id = lax.broadcasted_iota(jnp.int32, (n, n), 0)
    col_id = lax.broadcasted_iota(jnp.int32, (n, n), 1)
    upper_ref[:LANES, :LANES] = gram_ref[:LANES]
    upper_ref[:LANES, LANES:] = gram_ref[LANES : 2 * LANES]
    upper_ref[LANES:, LANES:] = gram_ref[2 * LANES :]
    inverse_ref[...] = jnp.where(row_id == col_id, 1.0, 0.0)
    for top in range(0, n, PANEL):
        t0 = top // LANES
        cols = list(range(t0, tiles)) + [tiles + t for t in range(t0 + 1)]
        rows_of = lambda g: slice(top + SUB * g, top + SUB * (g + 1))
        lanes_of = lambda t: slice(LANES * (t % tiles), LANES * (t % tiles + 1))
        ref_of = lambda t: upper_ref if t < tiles else inverse_ref
        grp = [[ref_of(t)[rows_of(g), lanes_of(t)] for t in cols] for g in range(groups)]
        pivots = [jnp.ones((SUB, LANES), jnp.float32) for _ in range(groups)]
        for g0 in range(groups):
            c0 = (top + SUB * g0) % LANES
            heads = [[from_lane(grp[g][0], c0 + j) for j in range(SUB)] for g in range(g0, groups)]
            for i in range(SUB):
                pivot = from_row(heads[0][i], i)
                pivots[g0] = jnp.where(sub == i, pivot, pivots[g0])
                inverse = pl.reciprocal(pivot, approx=True)
                head_row = {j: from_row(heads[0][j], i) for j in range(i + 1, SUB)}
                row = [from_row(v, i) for v in grp[g0]]
                for g in range(g0, groups):
                    head = heads[g - g0]
                    factor = head[i] * inverse
                    if g == g0:
                        factor = jnp.where(sub > i, factor, 0.0)
                    for j in range(i + 1, SUB):
                        head[j] = head[j] - factor * head_row[j]
                    grp[g] = [v - factor * r for v, r in zip(grp[g], row)]
        for g in range(groups):
            scale = refine_rsqrt(pivots[g])
            for v, t in zip(grp[g], cols):
                v = v * scale
                if t < tiles:
                    v = jnp.where(lane + LANES * t >= sub + (top + SUB * g), v, 0.0)
                ref_of(t)[rows_of(g), lanes_of(t)] = v
        for t in range(t0):
            upper_ref[top : top + PANEL, lanes_of(t)] = jnp.zeros((PANEL, LANES), jnp.float32)
        below = top + PANEL
        if below < n:
            lo, hi = LANES * t0, LANES * (t0 + 1)
            first = below // LANES * LANES
            rows = jnp.concatenate([upper_ref[top:below, lo:], inverse_ref[top:below, :hi]], axis=1)
            update = full_product(upper_ref[top:below, first:], rows)[below - first :]
            upper_ref[below:, lo:] = upper_ref[below:, lo:] - update[:, : n - lo]
            inverse_ref[below:, :hi] = inverse_ref[below:, :hi] - update[:, n - lo :]


def cholesky(packed):
    n = RANK
    return pl.pallas_call(
        cholesky_kernel,
        out_shape=[f32(n, n)] * 2,
        compiler_params=pltpu.CompilerParams(vmem_limit_bytes=VMEM_LIMIT),
        cost_estimate=pl.CostEstimate(flops=64 * n * n * n, bytes_accessed=12 * n * n, transcendentals=n),
        name="cholesky256",
    )(packed)


def core_kernel(place_ref, below, upper, inverse, own_h, own_l, even_h, even_l, odd_h, odd_l, *rest):
    factor_ref, out_ref, weights = rest

    @pl.when(pl.program_id(0) == 0)
    def _():
        left = upper[...]
        right = rows_dot(inverse[...], below[...], HIGHEST)
        squares = jnp.sum(left * left, axis=1, keepdims=True) + jnp.sum(right * right, axis=1, keepdims=True)
        length = jnp.sqrt(squares)
        left, right = left / length, right / length
        factor_ref[...] = jnp.concatenate([left, right], axis=1).T
        low = place_ref[0] < 4
        own = jnp.where(low, left, right)
        other = jnp.where(low, right, left)
        n = RANK // 4
        first = jnp.concatenate([other[:, :n], other[:, 2 * n : 3 * n]], axis=1)
        second = jnp.concatenate([other[:, n : 2 * n], other[:, 3 * n :]], axis=1)
        first_even = (place_ref[0] & 1) == 0
        even = jnp.where(first_even, first, second)
        odd = jnp.where(first_even, second, first)
        high, small = split(jnp.concatenate([own, even, odd], axis=1))
        weights[...] = jnp.concatenate([high, small, high], axis=1)

    w = weights[...]
    cells = []
    for t in range(own_h.shape[0]):
        high = [r[t] for r in (own_h, even_h, odd_h)]
        small = [r[t] for r in (own_l, even_l, odd_l)]
        both = jnp.dot(w, jnp.concatenate(high + high + small, axis=0), preferred_element_type=jnp.float32)
        cells += [both[:, :LANES], both[:, LANES:]]
    out_ref[:, 0, :, :] = jnp.swapaxes(jnp.stack(cells, axis=0), 0, 1)


def core_and_factor(place, kept, streamed, ny, nz, fields):
    size = sum(x.shape[1] for x in streamed) // 2
    return pl.pallas_call(
        core_kernel,
        grid=(ny,),
        in_specs=[pl.BlockSpec(memory_space=pltpu.SMEM)]
        + [whole(x.shape) for x in kept]
        + [parts_of(x, nz // 2) for x in streamed],
        out_specs=[whole((size, RANK)), pl.BlockSpec((RANK, 1, nz, fields), lambda i: (0, i, 0, 0))],
        out_shape=[f32(size, RANK), f32(RANK, ny, nz, fields)],
        scratch_shapes=[pltpu.VMEM((RANK, 3 * size), jnp.bfloat16)],
        compiler_params=pltpu.CompilerParams(vmem_limit_bytes=VMEM_LIMIT),
        cost_estimate=pl.CostEstimate(
            flops=6 * size * RANK * ny * nz * fields,
            bytes_accessed=4 * (size + RANK) * ny * nz * fields,
            transcendentals=0,
        ),
        name="core",
    )(place, *kept, *streamed)


def tie(x, *deps):
    return lax.optimization_barrier((x,) + deps)[0]


def block_for(snapshot, device, nz):
    rows, ny, _, fields = snapshot.shape
    cut = lax.dynamic_slice_in_dim(snapshot, device * nz, nz, axis=2)
    return cut.transpose(1, 2, 0, 3).reshape(ny * nz, rows, fields)


def on_device_blocks(snapshot, wide, narrow):
    ny, nz = snapshot.shape[1], snapshot.shape[2] // wide
    here = lax.axis_index("wide")
    place = here.astype(jnp.int32).reshape(1)
    first = block_for(snapshot, here ^ 6, nz)
    snapshot = tie(snapshot, first)
    got = {}
    send = lambda k, *deps: over(("wide", wide, k))(tie(block_for(snapshot, here ^ k, nz), *deps))
    got[6] = over(("wide", wide, 6))(first)
    got[4], got[2], got[1] = send(4), send(2), send(1)
    got[3] = send(3, got[6])
    split_at = (ny - LATE) * nz
    blocks, late = {}, {}
    for k, after in ((5, 6), (7, 4)):
        block = tie(block_for(snapshot, here ^ k, nz), got[after])
        got[k] = over(("wide", wide, k))(block[:split_at])
        blocks[k] = block[split_at:]
    late[5] = over(("wide", wide, 5))(tie(blocks[5], got[7]))
    late[7] = over(("wide", wide, 7))(tie(blocks[7], got[7]))
    got[0] = block_for(snapshot, here, nz)
    own_gram, *own = gram_of_own(place, [got[k] for k in range(4)], ny)
    cross_even, gram_even, *even = gram_of_even(place, got[4], got[6], own, ny)
    all_odd, *odd = gram_of_odd(place, got[5], got[7], own, even, ny - LATE)
    kept = [own_gram, cross_even, gram_even, all_odd]
    corner, below, *odd = gram_of_last(place, kept, late[5], late[7], own, even, odd, LATE * LATE_STEPS)
    corner, below = sum_both(corner, below, wide, narrow)
    upper, inverse = cholesky(corner)
    factor, core = core_and_factor(
        place, [below, upper, inverse], [*own, *even, *odd], ny, nz, snapshot.shape[3]
    )
    return core, factor


def on_device_any(snapshot):
    regrouped = lax.all_to_all(snapshot, "wide", split_axis=2, concat_axis=0, tiled=True)
    rows_all = regrouped.shape[0]
    unfold = regrouped.reshape(rows_all, -1)
    gram = lax.dot_general(
        unfold, unfold[:RANK], (((1,), (1,)), ((), ())), precision=HIGHEST, preferred_element_type=jnp.float32
    )
    gram = lax.psum(lax.psum(gram, "narrow"), "wide")
    lower = jnp.linalg.cholesky(gram[:RANK])
    upper = jnp.concatenate(
        [lower.T, lax.linalg.triangular_solve(lower, gram[RANK:].T, left_side=True, lower=True)], axis=1
    )
    lengths = jnp.sqrt(jnp.sum(upper * upper, axis=1))
    factor = (upper / lengths[:, None]).T
    core = jnp.dot(factor.T, unfold, precision=HIGHEST, preferred_element_type=jnp.float32)
    return core.reshape((RANK,) + regrouped.shape[1:]), factor


def solution(mesh):
    wide, narrow = mesh.shape["wide"], mesh.shape["narrow"]
    if (wide, narrow) == (FAST_WIDE, FAST_NARROW):
        on_device = functools.partial(on_device_blocks, wide=wide, narrow=narrow)
    else:
        on_device = on_device_any
    return jax.shard_map(
        on_device,
        mesh=mesh,
        in_specs=(P("wide", "narrow", None, None),),
        out_specs=(P(None, "narrow", "wide", None), P()),
        check_vma=False,
    )
```

```python
import functools

import jax
import jax.numpy as jnp
from jax import lax
from jax.experimental import pallas as pl
from jax.experimental.pallas import tpu as pltpu
from jax.sharding import PartitionSpec as P

RANK = 256
LANES = 128
FAST_WIDE, FAST_NARROW = 8, 4
LATE = 1
LATE_STEPS = 1
HIGHEST = lax.Precision.HIGHEST
VMEM_LIMIT = 16 * 1024 * 1024


def split_off(x):
    high = x.astype(jnp.bfloat16)
    return high, x - high.astype(jnp.float32)


def split(x):
    high, rest = split_off(x)
    return high, rest.astype(jnp.bfloat16)


def by_device(place, blocks):
    distance = 1
    while distance < len(blocks):
        flag = (place & distance) != 0
        blocks = [jnp.where(flag, blocks[i ^ distance], blocks[i]) for i in range(len(blocks))]
        distance *= 2
    return blocks


def two_cells(place, refs, t):
    sides = [jnp.concatenate(by_device(place, [r[c] for r in refs]), axis=0) for c in (2 * t, 2 * t + 1)]
    return jnp.concatenate(sides, axis=1)


def rows_dot(a, b, precision=None):
    return lax.dot_general(
        a, b, (((1,), (1,)), ((), ())), precision=precision, preferred_element_type=jnp.float32
    )


def product(a, b):
    (ah, al), (bh, bl) = a, b
    left = jnp.concatenate([ah, ah, al, al], axis=1)
    right = jnp.concatenate([bh, bl, bh, bl], axis=1)
    return rows_dot(left, right)


def read(pair, t):
    return pair[0][t], pair[1][t]


def write(pair, t, value):
    pair[0][t], pair[1][t] = value


def add_to(ref, value):
    ref[...] = ref[...] + value


def start_at_zero(*refs):
    @pl.when(pl.program_id(0) == 0)
    def _():
        for ref in refs:
            ref[...] = jnp.zeros_like(ref)


def own_kernel(place_ref, *refs):
    blocks, (gram_ref, *own) = refs[:-3], refs[-3:]
    start_at_zero(gram_ref)
    for t in range(blocks[0].shape[0] // 2):
        x = split(two_cells(place_ref[0], blocks, t))
        write(own, t, x)
        add_to(gram_ref, product(x, x))


def even_kernel(place_ref, near, far, own_h, own_l, cross_ref, gram_ref, *even):
    start_at_zero(cross_ref, gram_ref)
    place = place_ref[0] // 2
    for t in range(near.shape[0] // 2):
        x = split(two_cells(place, (near, far), t))
        write(even, t, x)
        add_to(cross_ref, product(x, read((own_h, own_l), t)))
        add_to(gram_ref, product(x, x))


def add_odd(place_ref, near, far, own, even, odd, all_ref):
    for t in range(near.shape[0] // 2):
        x = split(two_cells(place_ref[0] // 2, (near, far), t))
        write(odd, t, x)
        both = jnp.concatenate(x, axis=0)
        n = both.shape[0] // 2
        high = rows_dot(jnp.concatenate([own[0][t], even[0][t], x[0]], axis=0), both)
        low = rows_dot(jnp.concatenate([own[1][t], even[1][t], x[1]], axis=0), both)
        add_to(all_ref, (high[:, :n] + high[:, n:]) + (low[:, :n] + low[:, n:]))


def odd_kernel(place_ref, near, far, own_h, own_l, even_h, even_l, all_ref, odd_h, odd_l):
    start_at_zero(all_ref)
    add_odd(place_ref, near, far, (own_h, own_l), (even_h, even_l), (odd_h, odd_l), all_ref)


def last_kernel(
    place_ref, own_gram, cross_even, gram_even, all_odd, near, far, own_h, own_l, even_h, even_l, _, __,
    corner_ref, below_ref, odd_h, odd_l, all_ref,
):
    @pl.when(pl.program_id(0) == 0)
    def _():
        all_ref[...] = all_odd[...]

    add_odd(place_ref, near, far, (own_h, own_l), (even_h, even_l), (odd_h, odd_l), all_ref)
    place = place_ref[0]

    @pl.when(pl.program_id(0) == pl.num_programs(0) - 1)
    def _():
        n = all_ref.shape[1] // 2
        first_even = (place & 1) == 0

        def interleave(even, odd):
            a = jnp.where(first_even, even, odd)
            b = jnp.where(first_even, odd, even)
            return jnp.concatenate([a[:n], b[:n], a[n:], b[n:]], axis=0)

        low = place < FAST_WIDE // 2
        cross = interleave(cross_even[...], all_ref[:RANK].T)
        mixed = all_ref[RANK : RANK + 2 * n]
        other = interleave(
            jnp.concatenate([gram_even[...], mixed], axis=1),
            jnp.concatenate([mixed.T, all_ref[RANK + 2 * n :]], axis=1),
        ).T
        other = interleave(other[: 2 * n], other[2 * n :])
        corner = jnp.where(low, own_gram[...], other)
        corner_ref[...] = jnp.concatenate(
            [corner[:LANES, :LANES], corner[:LANES, LANES:], corner[LANES:, LANES:]], axis=0
        )
        below_ref[...] = jnp.where(low, cross, cross.T)


def whole(shape):
    return pl.BlockSpec(shape, lambda i: (0,) * len(shape))


def parts_of(x, size, first=0):
    return pl.BlockSpec((size,) + x.shape[1:], lambda i: (i + first,) + (0,) * (len(x.shape) - 1))


def call(
    kernel, name, steps, place, kept, blocks, split_blocks, kept_out, out, first=0, filled=(), scratch=(), flops=0
):
    pairs = blocks[0].shape[0] // 2 // steps
    moved = sum(4 * x.size for x in blocks) + sum(2 * s.size for s in out)
    return pl.pallas_call(
        kernel,
        grid=(steps,),
        in_specs=[pl.BlockSpec(memory_space=pltpu.SMEM)]
        + [whole(x.shape) for x in kept]
        + [parts_of(x, 2 * pairs) for x in blocks]
        + [parts_of(x, pairs, first) for x in split_blocks]
        + [pl.BlockSpec(memory_space=pl.ANY) for _ in filled],
        out_specs=[whole(s.shape) for s in kept_out] + [parts_of(s, pairs, first) for s in out],
        out_shape=list(kept_out) + list(out),
        scratch_shapes=list(scratch),
        input_output_aliases={
            1 + len(kept) + len(blocks) + len(split_blocks) + i: len(kept_out) + i for i in range(len(filled))
        },
        compiler_params=pltpu.CompilerParams(vmem_limit_bytes=VMEM_LIMIT),
        cost_estimate=pl.CostEstimate(flops=flops, bytes_accessed=moved, transcendentals=0),
        name=name,
    )(place, *kept, *blocks, *split_blocks, *filled)


def f32(*shape):
    return jax.ShapeDtypeStruct(shape, jnp.float32)


def halves(cells, rows, fields):
    return [jax.ShapeDtypeStruct((cells // 2, rows, 2 * fields), jnp.bfloat16)] * 2


def gram_of_own(place, blocks, steps):
    cells, rows, fields = blocks[0].shape
    n = rows * len(blocks)
    return call(
        own_kernel, "own_gram", steps, place, [], blocks, [], [f32(n, n)], halves(cells, n, fields),
        flops=8 * n * n * cells * fields,
    )


def gram_of_even(place, near, far, own, steps):
    cells, rows, fields = near.shape
    n = 2 * rows
    return call(
        even_kernel, "even_gram", steps, place, [], [near, far], own,
        [f32(n, 2 * n), f32(n, n)], halves(cells, n, fields), flops=24 * n * n * cells * fields,
    )


def gram_of_odd(place, near, far, own, even, steps):
    cells, rows, fields = near.shape
    n = 2 * rows
    return call(
        odd_kernel, "odd_gram", steps, place, [], [near, far], [*own, *even],
        [f32(4 * n, n)], halves(2 * own[0].shape[0], n, fields), flops=32 * n * n * cells * fields,
    )


def gram_of_last(place, kept, near, far, own, even, odd, steps):
    cells, rows, fields = near.shape
    n = 2 * rows
    pairs = cells // 2 // steps
    return call(
        last_kernel, "last_gram", steps, place, kept, [near, far], [*own, *even],
        [f32(3 * LANES, LANES), f32(RANK, RANK)], halves(2 * own[0].shape[0], n, fields), own[0].shape[0] // pairs - steps, odd,
        [pltpu.VMEM((4 * n, n), jnp.float32)], flops=32 * n * n * cells * fields,
    )


def over(step):
    axis, n, distance = step
    return functools.partial(lax.ppermute, axis_name=axis, perm=[(i, i ^ distance) for i in range(n)])


def sum_over_all(x, halved, doubled):
    sides = [(lax.axis_index(axis) & distance) != 0 for axis, _, distance in halved]
    for step, side in zip(halved, sides):
        n = x.shape[0] // 2
        keep = jnp.where(side, x[n:], x[:n])
        send = jnp.where(side, x[:n], x[n:])
        x = keep + over(step)(send)
    for step in doubled:
        x = x + over(step)(x)
    for step, side in reversed(list(zip(halved, sides))):
        got = over(step)(x)
        x = jnp.where(side, jnp.concatenate([got, x]), jnp.concatenate([x, got]))
    return x


def sum_both(corner, below, wide, narrow):
    core, y = ("narrow", narrow, 1), ("narrow", narrow, 2)
    x, z_near, z_far = [("wide", wide, 1 << b) for b in range(3)]
    corner = sum_over_all(corner, [core, z_near], [x, y, z_far])
    below = sum_over_all(below, [core, x], [z_near, z_far, y])
    return corner, below


PANEL = 64
SUB = 8


def refine_rsqrt(d):
    r = lax.rsqrt(d)
    return r * (1.5 - 0.5 * d * r * r)


def from_row(v, i):
    return jnp.broadcast_to(v[i : i + 1, :], (SUB, LANES))


def from_lane(v, c):
    return jnp.broadcast_to(v[:, c : c + 1], (SUB, LANES))


def full_product(a, b):
    def terms(x):
        high, rest = split_off(x)
        middle, rest = split_off(rest)
        return high, middle, rest.astype(jnp.bfloat16)

    (ah, am, al), (bh, bm, bl) = terms(a), terms(b)
    left = jnp.concatenate([ah, ah, am, ah, am, al], axis=0)
    right = jnp.concatenate([bh, bm, bh, bl, bm, bh], axis=0)
    return lax.dot_general(left, right, (((0,), (0,)), ((), ())), preferred_element_type=jnp.float32)


def cholesky_kernel(gram_ref, upper_ref, inverse_ref):
    n = upper_ref.shape[0]
    tiles = n // LANES
    groups = PANEL // SUB
    sub = lax.broadcasted_iota(jnp.int32, (SUB, LANES), 0)
    lane = lax.broadcasted_iota(jnp.int32, (SUB, LANES), 1)
    row_id = lax.broadcasted_iota(jnp.int32, (n, n), 0)
    col_id = lax.broadcasted_iota(jnp.int32, (n, n), 1)
    upper_ref[:LANES, :LANES] = gram_ref[:LANES]
    upper_ref[:LANES, LANES:] = gram_ref[LANES : 2 * LANES]
    upper_ref[LANES:, LANES:] = gram_ref[2 * LANES :]
    inverse_ref[...] = jnp.where(row_id == col_id, 1.0, 0.0)
    for top in range(0, n, PANEL):
        t0 = top // LANES
        cols = list(range(t0, tiles)) + [tiles + t for t in range(t0 + 1)]
        rows_of = lambda g: slice(top + SUB * g, top + SUB * (g + 1))
        lanes_of = lambda t: slice(LANES * (t % tiles), LANES * (t % tiles + 1))
        ref_of = lambda t: upper_ref if t < tiles else inverse_ref
        grp = [[ref_of(t)[rows_of(g), lanes_of(t)] for t in cols] for g in range(groups)]
        pivots = [jnp.ones((SUB, LANES), jnp.float32) for _ in range(groups)]
        for g0 in range(groups):
            c0 = (top + SUB * g0) % LANES
            heads = [[from_lane(grp[g][0], c0 + j) for j in range(SUB)] for g in range(g0, groups)]
            for i in range(SUB):
                pivot = from_row(heads[0][i], i)
                pivots[g0] = jnp.where(sub == i, pivot, pivots[g0])
                inverse = pl.reciprocal(pivot, approx=True)
                head_row = {j: from_row(heads[0][j], i) for j in range(i + 1, SUB)}
                row = [from_row(v, i) for v in grp[g0]]
                for g in range(g0, groups):
                    head = heads[g - g0]
                    factor = head[i] * inverse
                    if g == g0:
                        factor = jnp.where(sub > i, factor, 0.0)
                    for j in range(i + 1, SUB):
                        head[j] = head[j] - factor * head_row[j]
                    grp[g] = [v - factor * r for v, r in zip(grp[g], row)]
        for g in range(groups):
            scale = refine_rsqrt(pivots[g])
            for v, t in zip(grp[g], cols):
                v = v * scale
                if t < tiles:
                    v = jnp.where(lane + LANES * t >= sub + (top + SUB * g), v, 0.0)
                ref_of(t)[rows_of(g), lanes_of(t)] = v
        for t in range(t0):
            upper_ref[top : top + PANEL, lanes_of(t)] = jnp.zeros((PANEL, LANES), jnp.float32)
        below = top + PANEL
        if below < n:
            lo, hi = LANES * t0, LANES * (t0 + 1)
            first = below // LANES * LANES
            rows = jnp.concatenate([upper_ref[top:below, lo:], inverse_ref[top:below, :hi]], axis=1)
            update = full_product(upper_ref[top:below, first:], rows)[below - first :]
            upper_ref[below:, lo:] = upper_ref[below:, lo:] - update[:, : n - lo]
            inverse_ref[below:, :hi] = inverse_ref[below:, :hi] - update[:, n - lo :]


def cholesky(packed):
    n = RANK
    return pl.pallas_call(
        cholesky_kernel,
        out_shape=[f32(n, n)] * 2,
        compiler_params=pltpu.CompilerParams(vmem_limit_bytes=VMEM_LIMIT),
        cost_estimate=pl.CostEstimate(flops=64 * n * n * n, bytes_accessed=12 * n * n, transcendentals=n),
        name="cholesky256",
    )(packed)


def core_kernel(place_ref, below, upper, inverse, own_h, own_l, even_h, even_l, odd_h, odd_l, *rest):
    factor_ref, out_ref, weights = rest

    @pl.when(pl.program_id(0) == 0)
    def _():
        left = upper[...]
        right = rows_dot(inverse[...], below[...], HIGHEST)
        squares = jnp.sum(left * left, axis=1, keepdims=True) + jnp.sum(right * right, axis=1, keepdims=True)
        length = jnp.sqrt(squares)
        left, right = left / length, right / length
        factor_ref[...] = jnp.concatenate([left, right], axis=1).T
        low = place_ref[0] < 4
        own = jnp.where(low, left, right)
        other = jnp.where(low, right, left)
        n = RANK // 4
        first = jnp.concatenate([other[:, :n], other[:, 2 * n : 3 * n]], axis=1)
        second = jnp.concatenate([other[:, n : 2 * n], other[:, 3 * n :]], axis=1)
        first_even = (place_ref[0] & 1) == 0
        even = jnp.where(first_even, first, second)
        odd = jnp.where(first_even, second, first)
        high, small = split(jnp.concatenate([own, even, odd], axis=1))
        weights[...] = jnp.concatenate([high, small, high], axis=1)

    w = weights[...]
    cells = []
    for t in range(own_h.shape[0]):
        high = [r[t] for r in (own_h, even_h, odd_h)]
        small = [r[t] for r in (own_l, even_l, odd_l)]
        both = jnp.dot(w, jnp.concatenate(high + high + small, axis=0), preferred_element_type=jnp.float32)
        cells += [both[:, :LANES], both[:, LANES:]]
    out_ref[:, 0, :, :] = jnp.swapaxes(jnp.stack(cells, axis=0), 0, 1)


def core_and_factor(place, kept, streamed, ny, nz, fields):
    size = sum(x.shape[1] for x in streamed) // 2
    return pl.pallas_call(
        core_kernel,
        grid=(ny,),
        in_specs=[pl.BlockSpec(memory_space=pltpu.SMEM)]
        + [whole(x.shape) for x in kept]
        + [parts_of(x, nz // 2) for x in streamed],
        out_specs=[whole((size, RANK)), pl.BlockSpec((RANK, 1, nz, fields), lambda i: (0, i, 0, 0))],
        out_shape=[f32(size, RANK), f32(RANK, ny, nz, fields)],
        scratch_shapes=[pltpu.VMEM((RANK, 3 * size), jnp.bfloat16)],
        compiler_params=pltpu.CompilerParams(vmem_limit_bytes=VMEM_LIMIT),
        cost_estimate=pl.CostEstimate(
            flops=6 * size * RANK * ny * nz * fields,
            bytes_accessed=4 * (size + RANK) * ny * nz * fields,
            transcendentals=0,
        ),
        name="core",
    )(place, *kept, *streamed)


def tie(x, *deps):
    return lax.optimization_barrier((x,) + deps)[0]


def block_for(snapshot, device, nz):
    rows, ny, _, fields = snapshot.shape
    cut = lax.dynamic_slice_in_dim(snapshot, device * nz, nz, axis=2)
    return cut.transpose(1, 2, 0, 3).reshape(ny * nz, rows, fields)


def on_device_blocks(snapshot, wide, narrow):
    ny, nz = snapshot.shape[1], snapshot.shape[2] // wide
    here = lax.axis_index("wide")
    place = here.astype(jnp.int32).reshape(1)
    first = block_for(snapshot, here ^ 6, nz)
    snapshot = tie(snapshot, first)
    got = {}
    send = lambda k, *deps: over(("wide", wide, k))(tie(block_for(snapshot, here ^ k, nz), *deps))
    got[6] = over(("wide", wide, 6))(first)
    got[4], got[2], got[1] = send(4), send(2), send(1)
    got[3] = send(3, got[6])
    split_at = (ny - LATE) * nz
    blocks, late = {}, {}
    for k, after in ((5, 6), (7, 4)):
        block = tie(block_for(snapshot, here ^ k, nz), got[after])
        got[k] = over(("wide", wide, k))(block[:split_at])
        blocks[k] = block[split_at:]
    late[5] = over(("wide", wide, 5))(tie(blocks[5], got[7]))
    late[7] = over(("wide", wide, 7))(tie(blocks[7], got[7]))
    got[0] = block_for(snapshot, here, nz)
    own_gram, *own = gram_of_own(place, [got[k] for k in range(4)], ny)
    cross_even, gram_even, *even = gram_of_even(place, got[4], got[6], own, ny)
    all_odd, *odd = gram_of_odd(place, got[5], got[7], own, even, ny - LATE)
    kept = [own_gram, cross_even, gram_even, all_odd]
    corner, below, *odd = gram_of_last(place, kept, late[5], late[7], own, even, odd, LATE * LATE_STEPS)
    corner, below = sum_both(corner, below, wide, narrow)
    upper, inverse = cholesky(corner)
    factor, core = core_and_factor(
        place, [below, upper, inverse], [*own, *even, *odd], ny, nz, snapshot.shape[3]
    )
    return core, factor


def on_device_any(snapshot):
    regrouped = lax.all_to_all(snapshot, "wide", split_axis=2, concat_axis=0, tiled=True)
    rows_all = regrouped.shape[0]
    unfold = regrouped.reshape(rows_all, -1)
    gram = lax.dot_general(
        unfold, unfold[:RANK], (((1,), (1,)), ((), ())), precision=HIGHEST, preferred_element_type=jnp.float32
    )
    gram = lax.psum(lax.psum(gram, "narrow"), "wide")
    lower = jnp.linalg.cholesky(gram[:RANK])
    upper = jnp.concatenate(
        [lower.T, lax.linalg.triangular_solve(lower, gram[RANK:].T, left_side=True, lower=True)], axis=1
    )
    lengths = jnp.sqrt(jnp.sum(upper * upper, axis=1))
    factor = (upper / lengths[:, None]).T
    core = jnp.dot(factor.T, unfold, precision=HIGHEST, preferred_element_type=jnp.float32)
    return core.reshape((RANK,) + regrouped.shape[1:]), factor


def solution(mesh):
    wide, narrow = mesh.shape["wide"], mesh.shape["narrow"]
    if (wide, narrow) == (FAST_WIDE, FAST_NARROW):
        on_device = functools.partial(on_device_blocks, wide=wide, narrow=narrow)
    else:
        on_device = on_device_any
    return jax.shard_map(
        on_device,
        mesh=mesh,
        in_specs=(P("wide", "narrow", None, None),),
        out_specs=(P(None, "narrow", "wide", None), P()),
        check_vma=False,
    )
```
